512 devices in a mesh: span: 64 (over y_hi, z, core), seq: 8 (over x, y_lo).
Axes of the slice: x: 4, y: 4 (y_hi: 2, y_lo: 2; y = y_hi * 2 + y_lo), z: 16, core: 2. Of those that a mesh axis runs over, the one named last changes fastest.
Arguments:
- queries: bfloat16 [64, 128, 3072], P('span', 'seq'), may hold values from -16 to 16
- key_value_pairs: bfloat16 [64, 128, 2048], P('span', 'seq'), may hold values from -16 to 16
- span_index: int32 [64], P('span'), may hold values from 0 to 63, each once
- valid_count: int32 [64], P('span'), may hold values from 32 to 128, as said below
Outputs:
- attended: bfloat16 [64, 128, 3072], P('span', 'seq')
The draws below stay inside these ranges and needn't reach their ends.
Inputs may be any that keep to these rules, and one draw needn't show every extreme that they name: `span_index`: a permutation of 0 to 63. `valid_count`: some span has all 128 slots valid.
All inputs are finite; a program needn't handle non-finite values.
Results may differ from the reference program's by a relative error of at most 0.035.
Values may be sent and summed in bfloat16 or wider, within the bound.
A program may use at most 128 MiB of HBM per device.

```python
import jax
import jax.numpy as jnp
from jax import lax

QUERY_HEAD_COUNT = 24
KEY_VALUE_GROUPS = 8
HEAD_SIZE = 128
SPAN_TOKENS = 128
SPANS_IN_FLIGHT = 64


def draw_queries(key, part):
    key = jax.random.fold_in(key, 11)
    values = 2.5 * jnp.clip(jax.random.normal(key, (SPANS_IN_FLIGHT, SPAN_TOKENS, QUERY_HEAD_COUNT * HEAD_SIZE), jnp.float32), -4.8, 4.8)
    return values.astype(jnp.bfloat16)


def draw_key_value_pairs(key, part):
    key = jax.random.fold_in(key, 23)
    first, second = jax.random.split(key)
    target_shape = (SPANS_IN_FLIGHT, SPAN_TOKENS, KEY_VALUE_GROUPS, HEAD_SIZE)
    key_part = jnp.clip(jax.random.normal(first, target_shape, jnp.float32), -6.0, 6.0)
    value_part = 2.0 * jnp.clip(jax.random.normal(second, target_shape, jnp.float32), -6.0, 6.0)
    stacked_rows = jnp.stack([key_part, value_part], axis=3)
    return stacked_rows.reshape(SPANS_IN_FLIGHT, SPAN_TOKENS, KEY_VALUE_GROUPS * 2 * HEAD_SIZE).astype(jnp.bfloat16)


def draw_valid_count(key, part):
    key = jax.random.fold_in(key, 31)
    first, second = jax.random.split(key)
    counts = jax.random.randint(first, (SPANS_IN_FLIGHT,), SPAN_TOKENS // 4, SPAN_TOKENS + 1)
    chosen = jax.random.randint(second, (), 0, SPANS_IN_FLIGHT)
    return jnp.where(jnp.arange(SPANS_IN_FLIGHT) == chosen, SPAN_TOKENS, counts).astype(jnp.int32)


def setup_inputs(seed: int = 0) -> dict:
    key_list = jax.random.split(jax.random.key(seed), 5)
    return {
        "queries": draw_queries(jax.random.fold_in(key_list[4], 71), 0),
        "key_value_pairs": draw_key_value_pairs(jax.random.fold_in(key_list[4], 71), 0),
        "span_index": jax.random.permutation(key_list[2], SPANS_IN_FLIGHT).astype(jnp.int32),
        "valid_count": draw_valid_count(jax.random.fold_in(key_list[4], 71), 0),
    }


NEG = -1.0e30


def reference(queries, key_value_pairs, span_index, valid_count):
    group_list = QUERY_HEAD_COUNT // KEY_VALUE_GROUPS
    split_parts = key_value_pairs.reshape(SPANS_IN_FLIGHT * SPAN_TOKENS, KEY_VALUE_GROUPS, 2, HEAD_SIZE)
    key_rows = split_parts[:, :, 0].astype(jnp.float32)
    value_rows = split_parts[:, :, 1].astype(jnp.float32)
    slots = jnp.arange(SPAN_TOKENS, dtype=jnp.int32)
    slot_valid = (slots[None, :] < valid_count[:, None]).reshape(-1)
    slot_span = jnp.repeat(span_index, SPAN_TOKENS)
    score_scale = HEAD_SIZE ** -0.5

    def per_span(current_span):
        query_head_groups = queries[current_span].reshape(SPAN_TOKENS, KEY_VALUE_GROUPS, group_list, HEAD_SIZE).astype(jnp.float32)
        visible = slot_valid & (slot_span <= span_index[current_span])

        def heads_per_group(group):
            scores = jnp.einsum("tgd,ud->gtu", query_head_groups[:, group], key_rows[:, group]) * score_scale
            scores = jnp.where(visible, scores, NEG)
            row_max = jnp.max(scores, axis=-1, keepdims=True)
            raw = jnp.where(visible, jnp.exp(scores - row_max), 0.0)
            total = jnp.sum(raw, axis=-1)
            rounded = lax.optimization_barrier(raw.astype(jnp.bfloat16)).astype(jnp.float32)
            summed = jnp.einsum("gtu,ud->gtd", rounded, value_rows[:, group])
            return (summed / total[..., None]).astype(jnp.bfloat16)

        attention_output = lax.map(heads_per_group, jnp.arange(KEY_VALUE_GROUPS))
        return attention_output.transpose(2, 0, 1, 3).reshape(SPAN_TOKENS, QUERY_HEAD_COUNT * HEAD_SIZE)

    return lax.map(per_span, jnp.arange(SPANS_IN_FLIGHT))
```

```python
import functools
import math

import jax
import jax.numpy as jnp
from jax import lax
from jax.experimental import pallas as pl
from jax.experimental.pallas import tpu as pltpu
from jax.sharding import PartitionSpec as P

MESH = pl.DeviceIdType.MESH
HEAD = 128
LIST = 3
KEYS = 128
META = 16
ROW_EXTRA = 128
SCALE = HEAD ** (-0.5) / math.log(2.0)
NO_MAX = -(2.0**100)
HIDDEN = -(2.0**101)
FAR = 100.0


def kernel(
    n_span, n_seq,
    q_hbm, kv_hbm, index_ref, count_ref, out_ref,
    kbuf, vbuf, qbuf, own_meta, partner_meta, max_ref, sum_ref, acc_ref, part_buf, got_buf,
    a2a_send, a2a_recv, ring_send, k_recv, v_recv,
):
    tokens = q_hbm.shape[1]
    half_spans = n_span // 2
    n_z = half_spans // 2
    span = lax.axis_index("span")
    seq = lax.axis_index("seq")
    half = lax.div(span, half_spans)
    slot = lax.rem(span, half_spans)
    z = lax.div(slot, 2)
    core = lax.rem(slot, 2)
    group = seq ^ half
    partner_span = (1 - half) * half_spans + slot
    sibling = (half * half_spans + z * 2 + (1 - core), seq)

    def z_at(offset):
        return lax.rem(z + offset + n_z, n_z)

    up = (half * half_spans + z_at(1) * 2 + core, seq)
    down = (half * half_spans + z_at(-1) * 2 + core, seq)

    barrier = pltpu.get_barrier_semaphore()
    for d in range(1, n_seq):
        pl.semaphore_signal(barrier, inc=1, device_id=(span, seq ^ d), device_id_type=MESH)
    for d in range(n_seq):
        pl.semaphore_signal(barrier, inc=1, device_id=(partner_span, seq ^ d), device_id_type=MESH)
    for device in (up, down, sibling):
        pl.semaphore_signal(barrier, inc=1, device_id=device, device_id_type=MESH)
    pl.semaphore_wait(barrier, 2 * n_seq + 2)

    def send(src, dst, send_sem, recv_sem, device):
        pltpu.make_async_remote_copy(
            src_ref=src, dst_ref=dst, send_sem=send_sem, recv_sem=recv_sem, device_id=device, device_id_type=MESH
        ).start()

    def wait(ref, sem):
        pltpu.make_async_copy(ref, ref, sem).wait()

    rows = pl.ds(pl.multiple_of(seq * tokens, tokens), tokens)

    def columns(start, size):
        return pl.ds(pl.multiple_of(start, 128), size)

    for part, buf in ((0, kbuf), (1, vbuf)):
        for d in range(n_seq):
            their = (seq ^ d) ^ half
            src = kv_hbm.at[0, :, columns(their * 256 + part * 128, 128)]
            dst = buf.at[slot, rows, :]
            if d == 0:
                pltpu.make_async_copy(src, dst, a2a_recv.at[part]).start()
            else:
                send(src, dst, a2a_send.at[part], a2a_recv.at[part], (span, seq ^ d))

    for d in range(n_seq):
        their = (seq ^ d) ^ half
        src = q_hbm.at[0, :, columns(their * (LIST * HEAD), LIST * HEAD)]
        dst = qbuf.at[0, rows, :]
        if d == 0:
            pltpu.make_async_copy(src, dst, a2a_recv.at[2]).start()
        else:
            send(src, dst, a2a_send.at[2], a2a_recv.at[2], (span, seq ^ d))
    for d in range(n_seq):
        their = (seq ^ d) ^ (1 - half)
        src = q_hbm.at[0, :, columns(their * (LIST * HEAD), LIST * HEAD)]
        send(src, qbuf.at[1, rows, :], a2a_send.at[3], a2a_recv.at[3], (partner_span, seq ^ d))

    index = index_ref[0].astype(jnp.float32)
    count = count_ref[0]
    lane = lax.broadcasted_iota(jnp.int32, (META, 128), 1)
    kbuf[slot, KEYS:, :] = jnp.where(lane < count, index, FAR).astype(jnp.bfloat16)
    own_meta[...] = jnp.full((META, 128), index, jnp.float32).astype(jnp.bfloat16)
    send(own_meta, partner_meta, a2a_send.at[4], a2a_recv.at[4], (partner_span, seq ^ 1))

    max_ref[...] = jnp.full(max_ref.shape, NO_MAX, jnp.float32)
    sum_ref[...] = jnp.zeros(sum_ref.shape, jnp.float32)
    acc_ref[...] = jnp.zeros(acc_ref.shape, jnp.float32)

    def pass_on(buf, recv, send_sem, which, device):
        send(buf.at[which], buf.at[which], send_sem, recv.at[which], device)

    def pass_k(which, device):
        pass_on(kbuf, k_recv, ring_send.at[0], which, device)

    def pass_v(which, device):
        pass_on(vbuf, v_recv, ring_send.at[1], which, device)

    def wait_k(which):
        wait(kbuf.at[which], k_recv.at[which])

    def wait_v(which):
        wait(vbuf.at[which], v_recv.at[which])

    wait(kbuf.at[slot, pl.ds(0, KEYS), :], a2a_recv.at[0])
    for device in (up, down, sibling):
        pass_k(slot, device)
    wait(vbuf.at[slot], a2a_recv.at[1])
    for device in (up, down, sibling):
        pass_v(slot, device)

    def update(b, head, places):
        tile = b * LIST + head
        query = qbuf[b, :, head * HEAD : (head + 1) * HEAD]
        if b == 0:
            mine = own_meta[...].astype(jnp.float32)[:1]
        else:
            mine = partner_meta[...].astype(jnp.float32)[:1]
        scores = []
        for place in places:
            pair = pl.ds(place * 2, 2)
            keys = kbuf[pair, :KEYS, :].reshape(2 * KEYS, HEAD)
            meta = kbuf[pair, KEYS:, :].astype(jnp.float32)
            product = lax.dot_general(
                query, keys, (((1,), (1,)), ((), ())), preferred_element_type=jnp.float32
            )
            for i in range(2):
                bias = jnp.where(meta[i, :1] <= mine, 0.0, HIDDEN)
                scores.append(product[:, i * KEYS : (i + 1) * KEYS] * SCALE + bias)
        top = functools.reduce(jnp.maximum, scores)
        old_max = max_ref[tile]
        new_max = jnp.maximum(old_max, jnp.max(top, axis=-1, keepdims=True))
        alpha = jnp.exp2(old_max - new_max)
        raw = [jnp.exp2(s - new_max) for s in scores]
        max_ref[tile] = new_max
        sum_ref[tile] = sum_ref[tile] * alpha + functools.reduce(jnp.add, raw)
        total = acc_ref[tile] * alpha
        for i, place in enumerate(places):
            values = vbuf[pl.ds(place * 2, 2)].reshape(2 * KEYS, HEAD)
            weights = jnp.concatenate(raw[2 * i : 2 * i + 2], axis=1).astype(jnp.bfloat16)
            total += jnp.dot(weights, values, preferred_element_type=jnp.float32)
        acc_ref[tile] = total

    def wait_other(place):
        wait_k(place * 2 + 1 - core)
        wait_v(place * 2 + 1 - core)

    def own(place):
        return place * 2 + core

    def step(h, places, first=False):
        def tiles(*which):
            for i in which:
                update(i // LIST, i % LIST, places)

        before, after = own(z_at(-h)), own(z_at(h))
        wait_k(before)
        pass_k(before, up)
        pass_k(before, sibling)
        if first:
            wait(qbuf.at[0], a2a_recv.at[2])
            wait(qbuf.at[1], a2a_recv.at[3])
            wait(partner_meta, a2a_recv.at[4])
        for place in places:
            wait_other(place)
        tiles(0, 1)
        wait_k(after)
        pl.when(h < n_z // 2 - 1)(lambda: pass_k(after, down))
        pass_k(after, sibling)
        tiles(2)
        wait_v(before)
        pl.when(h < n_z // 2 - 1)(lambda: pass_v(before, up))
        pass_v(before, sibling)
        tiles(3, 4)
        wait_v(after)
        pass_v(after, down)
        pass_v(after, sibling)
        tiles(5)

    step(1, [z], first=True)

    def loop(h, carry):
        step(h, [z_at(1 - h), z_at(h - 1)])
        return carry

    lax.fori_loop(2, n_z // 2, loop, 0)

    last = z_at(n_z // 2)
    places = [z_at(1 - n_z // 2), z_at(n_z // 2 - 1)]
    wait_k(own(last))
    pass_k(own(last), sibling)
    for place in places:
        wait_other(place)
    for i in range(3):
        update(i // LIST, i % LIST, places)
    wait_v(own(last))
    pass_v(own(last), sibling)
    for i in range(3, 6):
        update(i // LIST, i % LIST, places)
    wait_other(last)
    lane = lax.broadcasted_iota(jnp.int32, (KEYS, 128), 1)
    for b in (1, 0):
        stats = jnp.zeros((KEYS, 128), jnp.float32)
        for head in range(LIST):
            update(b, head, [last])
            tile = b * LIST + head
            top = max_ref[tile]
            sent_max = top.astype(jnp.bfloat16).astype(jnp.float32)
            factor = jnp.exp2(top - sent_max)
            total = jnp.sum(sum_ref[tile], axis=-1, keepdims=True) * factor
            high = total.astype(jnp.bfloat16).astype(jnp.float32)
            stats = jnp.where(lane == 3 * head, sent_max, stats)
            stats = jnp.where(lane == 3 * head + 1, high, stats)
            stats = jnp.where(lane == 3 * head + 2, total - high, stats)
            part_buf[b, :, head * HEAD : (head + 1) * HEAD] = (acc_ref[tile] * factor).astype(jnp.bfloat16)
        part_buf[b, :, LIST * HEAD :] = stats.astype(jnp.bfloat16)
        for d in range(n_seq):
            to = seq ^ d
            src = part_buf.at[b, pl.ds(pl.multiple_of(to * tokens, tokens), tokens), :]
            dst = got_buf.at[b, group]
            if b == 0 and d == 0:
                pltpu.make_async_copy(src, dst, a2a_recv.at[5]).start()
            else:
                device = (span if b == 0 else partner_span, to)
                send(src, dst, a2a_send.at[5 + b], a2a_recv.at[5 + b], device)

    wait(kbuf.at[pl.ds(0, half_spans - 1)], ring_send.at[0])
    wait(vbuf.at[pl.ds(0, half_spans - 1)], ring_send.at[1])
    wait(vbuf.at[0, pl.ds(0, (n_seq - 1) * tokens), :], a2a_send.at[0])
    wait(vbuf.at[0, pl.ds(0, (n_seq - 1) * tokens), :], a2a_send.at[1])
    wait(qbuf.at[0, pl.ds(0, (n_seq - 1) * tokens), :], a2a_send.at[2])
    wait(qbuf.at[1], a2a_send.at[3])
    wait(own_meta, a2a_send.at[4])

    wait(got_buf.at[1], a2a_recv.at[6])
    wait(got_buf.at[0], a2a_recv.at[5])
    for g in range(n_seq):
        stats = [got_buf[b, g, :, LIST * HEAD :].astype(jnp.float32) for b in range(2)]
        for head in range(LIST):
            tops = [s[:, 3 * head : 3 * head + 1] for s in stats]
            totals = [s[:, 3 * head + 1 : 3 * head + 2] + s[:, 3 * head + 2 : 3 * head + 3] for s in stats]
            top = jnp.maximum(*tops)
            shares = [jnp.exp2(t - top) for t in tops]
            whole = shares[0] * totals[0] + shares[1] * totals[1]
            shares = [s / whole for s in shares]
            parts = [got_buf[b, g, :, head * HEAD : (head + 1) * HEAD].astype(jnp.float32) for b in range(2)]
            place = (g * LIST + head) * HEAD
            out_ref[0, :, place : place + HEAD] = (parts[0] * shares[0] + parts[1] * shares[1]).astype(jnp.bfloat16)
    wait(part_buf.at[0, pl.ds(0, (n_seq - 1) * tokens), :], a2a_send.at[5])
    wait(part_buf.at[1], a2a_send.at[6])


def solution(mesh):
    n_span, n_seq = mesh.shape["span"], mesh.shape["seq"]
    slots = n_span // 2

    def shards(queries, key_value_pairs, span_index, valid_count):
        tokens = queries.shape[1]
        return pl.pallas_call(
            functools.partial(kernel, n_span, n_seq),
            out_shape=jax.ShapeDtypeStruct(queries.shape, jnp.bfloat16),
            in_specs=[pl.BlockSpec(memory_space=pl.ANY)] * 2 + [pl.BlockSpec(memory_space=pltpu.SMEM)] * 2,
            out_specs=pl.BlockSpec(memory_space=pltpu.VMEM),
            scratch_shapes=[
                pltpu.VMEM((slots, KEYS + META, HEAD), jnp.bfloat16),
                pltpu.VMEM((slots, KEYS, HEAD), jnp.bfloat16),
                pltpu.VMEM((2, KEYS, LIST * HEAD), jnp.bfloat16),
                pltpu.VMEM((META, 128), jnp.bfloat16),
                pltpu.VMEM((META, 128), jnp.bfloat16),
                pltpu.VMEM((2 * LIST, KEYS, HEAD), jnp.float32),
                pltpu.VMEM((2 * LIST, KEYS, HEAD), jnp.float32),
                pltpu.VMEM((2 * LIST, KEYS, HEAD), jnp.float32),
                pltpu.VMEM((2, KEYS, LIST * HEAD + ROW_EXTRA), jnp.bfloat16),
                pltpu.VMEM((2, n_seq, tokens, LIST * HEAD + ROW_EXTRA), jnp.bfloat16),
                pltpu.SemaphoreType.DMA((7,)),
                pltpu.SemaphoreType.DMA((7,)),
                pltpu.SemaphoreType.DMA((2,)),
                pltpu.SemaphoreType.DMA((slots,)),
                pltpu.SemaphoreType.DMA((slots,)),
            ],
            compiler_params=pltpu.CompilerParams(
                collective_id=0, has_side_effects=True, vmem_limit_bytes=32 * 1024 * 1024
            ),
        )(queries, key_value_pairs, span_index, valid_count)

    return jax.shard_map(
        shards,
        mesh=mesh,
        in_specs=(P("span", "seq", None), P("span", "seq", None), P("span"), P("span")),
        out_specs=P("span", "seq", None),
        check_vma=False,
    )
```

```python
import functools
import math

import jax
import jax.numpy as jnp
from jax import lax
from jax.experimental import pallas as pl
from jax.experimental.pallas import tpu as pltpu
from jax.sharding import PartitionSpec as P

MESH = pl.DeviceIdType.MESH
HEAD = 128
LIST = 3
KEYS = 128
META = 16
ROW_EXTRA = 128
SCALE = HEAD ** (-0.5) / math.log(2.0)
NO_MAX = -(2.0**100)
HIDDEN = -(2.0**101)
FAR = 100.0


TREES = (
    {-7: -6, -6: -5, -5: -1, -4: -5, -3: -2, -2: -1, -1: 0, 1: 0, 2: 0, 3: 2, 4: 1, 5: 4, 6: 4, 7: 5, 8: -6},
    {-7: -6, -6: -4, -5: -4, -4: 0, -3: -4, -2: -3, -1: 0, 1: 2, 2: 0, 3: 0, 4: 3, 5: 4, 6: 3, 7: 6, 8: -5},
)
GROUPS = ((0, -1), (2, 3), (-5, 4), (1, -3), (-6, -4), (-2, 6), (5, -7), (8, 7))
EVENTS = (
    ((0, -1), (0, 1), (1, -1), (0, 2),),
    (),
    ((1, -4), (1, 2), (1, 3), (0, -2), (0, 4), (0, -5), (0, 3), (1, -5), (1, -3), (1, 4), (1, 1),),
    (),
    ((1, -6), (0, -3),),
    (),
    ((0, 5), (0, -6), (1, 6),),
    (),
    ((0, -4), (1, 8), (1, -2), (1, -7), (0, 6),),
    ((1, 5),),
    ((0, -7),),
    ((1, 7),),
    ((0, 8),),
    ((0, 7),),
    (),
)
CHILDREN = tuple(
    {parent: [child for child in tree if tree[child] == parent] for parent in set(tree.values())} for tree in TREES
)


def hops(child, parent):
    return (child - parent + 8) % 16 - 8


def kernel(
    n_span, n_seq,
    q_hbm, kv_hbm, index_hbm, count_hbm, out_ref,
    kbuf, vbuf, qbuf, place_buf, max_ref, sum_ref, acc_ref, part_buf, got_buf, index_smem, count_smem,
    a2a_send, a2a_recv, ring_send, k_recv, v_recv, int_sem,
):
    tokens = q_hbm.shape[1]
    half_spans = n_span // 2
    n_z = half_spans // 2
    span = lax.axis_index("span")
    seq = lax.axis_index("seq")
    half = lax.div(span, half_spans)
    slot = lax.rem(span, half_spans)
    z = lax.div(slot, 2)
    core = lax.rem(slot, 2)
    group = seq ^ half
    partner_span = (1 - half) * half_spans + slot
    sibling = (half * half_spans + z * 2 + (1 - core), seq)

    def z_at(offset):
        return lax.rem(z + offset + n_z, n_z)

    def along(offset):
        return (half * half_spans + z_at(offset) * 2 + core, seq)

    barrier = pltpu.get_barrier_semaphore()
    for d in range(1, n_seq):
        pl.semaphore_signal(barrier, inc=1, device_id=(span, seq ^ d), device_id_type=MESH)
    for d in range(n_seq):
        pl.semaphore_signal(barrier, inc=1, device_id=(partner_span, seq ^ d), device_id_type=MESH)
    steps = sorted({abs(hops(child, parent)) for tree in TREES for child, parent in tree.items()})
    for s in steps:
        for device in (along(s), along(-s)):
            pl.semaphore_signal(barrier, inc=1, device_id=device, device_id_type=MESH)
    pl.semaphore_signal(barrier, inc=1, device_id=sibling, device_id_type=MESH)

    ints = [
        pltpu.make_async_copy(index_hbm, index_smem, int_sem.at[0]),
        pltpu.make_async_copy(count_hbm, count_smem, int_sem.at[1]),
    ]
    for copy in ints:
        copy.start()
    max_ref[...] = jnp.full(max_ref.shape, NO_MAX, jnp.float32)
    sum_ref[...] = jnp.zeros(sum_ref.shape, jnp.float32)
    acc_ref[...] = jnp.zeros(acc_ref.shape, jnp.float32)
    for copy in ints:
        copy.wait()
    index = index_smem[0].astype(jnp.float32)
    lane = lax.broadcasted_iota(jnp.int32, (META, 128), 1)
    kbuf[slot, KEYS:, :] = jnp.where(lane < count_smem[0], index, FAR).astype(jnp.bfloat16)
    place_buf[0] = jnp.full((META, 128), index, jnp.float32).astype(jnp.bfloat16)

    pl.semaphore_wait(barrier, 2 * n_seq + 2 * len(steps))

    def send(src, dst, send_sem, recv_sem, device):
        pltpu.make_async_remote_copy(
            src_ref=src, dst_ref=dst, send_sem=send_sem, recv_sem=recv_sem, device_id=device, device_id_type=MESH
        ).start()

    def wait(ref, sem):
        pltpu.make_async_copy(ref, ref, sem).wait()

    rows = pl.ds(pl.multiple_of(seq * tokens, tokens), tokens)

    def columns(start, size):
        return pl.ds(pl.multiple_of(start, 128), size)

    for part, buf in ((0, kbuf), (1, vbuf)):
        for d in range(n_seq):
            their = (seq ^ d) ^ half
            src = kv_hbm.at[0, :, columns(their * 256 + part * 128, 128)]
            dst = buf.at[slot, rows, :]
            if d == 0:
                pltpu.make_async_copy(src, dst, a2a_recv.at[part]).start()
            else:
                send(src, dst, a2a_send.at[part], a2a_recv.at[part], (span, seq ^ d))

    for d in range(n_seq):
        their = (seq ^ d) ^ half
        src = q_hbm.at[0, :, columns(their * (LIST * HEAD), LIST * HEAD)]
        dst = qbuf.at[0, rows, :]
        if d == 0:
            pltpu.make_async_copy(src, dst, a2a_recv.at[2]).start()
        else:
            send(src, dst, a2a_send.at[2], a2a_recv.at[2], (span, seq ^ d))
    for d in range(n_seq):
        their = (seq ^ d) ^ (1 - half)
        src = q_hbm.at[0, :, columns(their * (LIST * HEAD), LIST * HEAD)]
        send(src, qbuf.at[1, rows, :], a2a_send.at[3], a2a_recv.at[3], (partner_span, seq ^ d))

    send(place_buf.at[0], place_buf.at[1], a2a_send.at[4], a2a_recv.at[4], (partner_span, seq ^ 1))

    bufs, recvs = (kbuf, vbuf), (k_recv, v_recv)

    def pass_on(chunk, which, device):
        send(bufs[chunk].at[which], bufs[chunk].at[which], ring_send.at[chunk], recvs[chunk].at[which], device)

    def wait_for(chunk, which):
        wait(bufs[chunk].at[which], recvs[chunk].at[which])

    def hand_on(chunk, offset):
        which = z_at(-offset) * 2 + core
        for child in CHILDREN[chunk].get(offset, ()):
            pass_on(chunk, which, along(hops(child, offset)))
        pass_on(chunk, which, sibling)

    wait(kbuf.at[slot, pl.ds(0, KEYS), :], a2a_recv.at[0])
    hand_on(0, 0)
    wait(vbuf.at[slot], a2a_recv.at[1])
    hand_on(1, 0)
    wait(qbuf.at[0], a2a_recv.at[2])
    wait(qbuf.at[1], a2a_recv.at[3])
    wait(place_buf.at[1], a2a_recv.at[4])

    def attend(b, places):
        mine = place_buf[b].astype(jnp.float32)[:1]
        pairs = [pl.ds(place * 2, 2) for place in places]
        metas = [kbuf[pair, KEYS:, :].astype(jnp.float32) for pair in pairs]
        biases = [jnp.where(meta[i, :1] <= mine, 0.0, HIDDEN) for meta in metas for i in range(2)]
        products = []
        for head in range(LIST):
            query = qbuf[b, :, head * HEAD : (head + 1) * HEAD]
            for pair in pairs:
                keys = kbuf[pair, :KEYS, :].reshape(2 * KEYS, HEAD)
                products.append(
                    lax.dot_general(query, keys, (((1,), (1,)), ((), ())), preferred_element_type=jnp.float32)
                )
        weights = []
        for head in range(LIST):
            tile = b * LIST + head
            scores = []
            for i, bias in enumerate(biases):
                product = products[head * len(pairs) + i // 2]
                scores.append(product[:, i % 2 * KEYS : (i % 2 + 1) * KEYS] * SCALE + bias)
            old_max = max_ref[tile]
            top = functools.reduce(jnp.maximum, scores)
            new_max = jnp.maximum(old_max, jnp.max(top, axis=-1, keepdims=True))
            alpha = jnp.exp2(old_max - new_max)
            raw = [jnp.exp2(score - new_max) for score in scores]
            max_ref[tile] = new_max
            sum_ref[tile] = sum_ref[tile] * alpha + functools.reduce(jnp.add, raw)
            weights.append((alpha, [w.astype(jnp.bfloat16) for w in raw]))
        for head in range(LIST):
            tile = b * LIST + head
            alpha, raw = weights[head]
            total = acc_ref[tile] * alpha
            for i, pair in enumerate(pairs):
                values = vbuf[pair].reshape(2 * KEYS, HEAD)
                total += jnp.dot(
                    jnp.concatenate(raw[2 * i : 2 * i + 2], axis=1), values, preferred_element_type=jnp.float32
                )
            acc_ref[tile] = total

    def finish(b):
        lane = lax.broadcasted_iota(jnp.int32, (KEYS, 128), 1)
        stats = jnp.zeros((KEYS, 128), jnp.float32)
        for head in range(LIST):
            tile = b * LIST + head
            top = max_ref[tile]
            sent_max = top.astype(jnp.bfloat16).astype(jnp.float32)
            factor = jnp.exp2(top - sent_max)
            total = jnp.sum(sum_ref[tile], axis=-1, keepdims=True) * factor
            high = total.astype(jnp.bfloat16).astype(jnp.float32)
            stats = jnp.where(lane == 3 * head, sent_max, stats)
            stats = jnp.where(lane == 3 * head + 1, high, stats)
            stats = jnp.where(lane == 3 * head + 2, total - high, stats)
            part_buf[b, :, head * HEAD : (head + 1) * HEAD] = (acc_ref[tile] * factor).astype(jnp.bfloat16)
        part_buf[b, :, LIST * HEAD :] = stats.astype(jnp.bfloat16)
        for d in range(n_seq):
            to = seq ^ d
            src = part_buf.at[b, pl.ds(pl.multiple_of(to * tokens, tokens), tokens), :]
            dst = got_buf.at[b, group]
            if b == 0 and d == 0:
                pltpu.make_async_copy(src, dst, a2a_recv.at[5]).start()
            else:
                device = (span if b == 0 else partner_span, to)
                send(src, dst, a2a_send.at[5 + b], a2a_recv.at[5 + b], device)

    def places_of(g):
        places = []
        for which in range(2):
            offset = GROUPS[0][which]
            for i in range(1, len(GROUPS)):
                offset = jnp.where(g == i, GROUPS[i][which], offset)
            places.append(z_at(-offset))
        return places

    def loop(i, carry):
        for at, events in enumerate(EVENTS):
            if events:

                @pl.when(i == at)
                def _():
                    for chunk, offset in events:
                        wait_for(chunk, z_at(-offset) * 2 + core)
                        hand_on(chunk, offset)

        places = places_of(lax.div(i, 2))

        @pl.when(lax.rem(i, 2) == 0)
        def _():
            for place in places:
                for chunk in range(2):
                    wait_for(chunk, place * 2 + 1 - core)

        attend(1 - lax.rem(i, 2), places)
        return carry

    lax.fori_loop(0, 2 * len(GROUPS) - 1, loop, 0)
    finish(1)
    attend(0, [z_at(-offset) for offset in GROUPS[-1]])
    finish(0)

    wait(kbuf.at[pl.ds(0, half_spans - 1)], ring_send.at[0])
    wait(vbuf.at[pl.ds(0, half_spans - 1)], ring_send.at[1])
    wait(vbuf.at[0, pl.ds(0, (n_seq - 1) * tokens), :], a2a_send.at[0])
    wait(vbuf.at[0, pl.ds(0, (n_seq - 1) * tokens), :], a2a_send.at[1])
    wait(qbuf.at[0, pl.ds(0, (n_seq - 1) * tokens), :], a2a_send.at[2])
    wait(qbuf.at[1], a2a_send.at[3])
    wait(place_buf.at[0], a2a_send.at[4])

    wait(got_buf.at[1], a2a_recv.at[6])
    wait(got_buf.at[0], a2a_recv.at[5])
    for g in range(n_seq):
        stats = [got_buf[b, g, :, LIST * HEAD :].astype(jnp.float32) for b in range(2)]
        for head in range(LIST):
            tops = [s[:, 3 * head : 3 * head + 1] for s in stats]
            totals = [s[:, 3 * head + 1 : 3 * head + 2] + s[:, 3 * head + 2 : 3 * head + 3] for s in stats]
            top = jnp.maximum(*tops)
            shares = [jnp.exp2(t - top) for t in tops]
            whole = shares[0] * totals[0] + shares[1] * totals[1]
            shares = [s / whole for s in shares]
            parts = [got_buf[b, g, :, head * HEAD : (head + 1) * HEAD].astype(jnp.float32) for b in range(2)]
            place = (g * LIST + head) * HEAD
            out_ref[0, :, place : place + HEAD] = (parts[0] * shares[0] + parts[1] * shares[1]).astype(jnp.bfloat16)
    wait(part_buf.at[0, pl.ds(0, (n_seq - 1) * tokens), :], a2a_send.at[5])
    wait(part_buf.at[1], a2a_send.at[6])


def solution(mesh):
    n_span, n_seq = mesh.shape["span"], mesh.shape["seq"]
    slots = n_span // 2

    def shards(queries, key_value_pairs, span_index, valid_count):
        tokens = queries.shape[1]
        return pl.pallas_call(
            functools.partial(kernel, n_span, n_seq),
            out_shape=jax.ShapeDtypeStruct(queries.shape, jnp.bfloat16),
            in_specs=[pl.BlockSpec(memory_space=pl.ANY)] * 4,
            out_specs=pl.BlockSpec(memory_space=pltpu.VMEM),
            scratch_shapes=[
                pltpu.VMEM((slots, KEYS + META, HEAD), jnp.bfloat16),
                pltpu.VMEM((slots, KEYS, HEAD), jnp.bfloat16),
                pltpu.VMEM((2, KEYS, LIST * HEAD), jnp.bfloat16),
                pltpu.VMEM((2, META, 128), jnp.bfloat16),
                pltpu.VMEM((2 * LIST, KEYS, HEAD), jnp.float32),
                pltpu.VMEM((2 * LIST, KEYS, HEAD), jnp.float32),
                pltpu.VMEM((2 * LIST, KEYS, HEAD), jnp.float32),
                pltpu.VMEM((2, KEYS, LIST * HEAD + ROW_EXTRA), jnp.bfloat16),
                pltpu.VMEM((2, n_seq, tokens, LIST * HEAD + ROW_EXTRA), jnp.bfloat16),
                pltpu.SMEM((1,), jnp.int32),
                pltpu.SMEM((1,), jnp.int32),
                pltpu.SemaphoreType.DMA((7,)),
                pltpu.SemaphoreType.DMA((7,)),
                pltpu.SemaphoreType.DMA((2,)),
                pltpu.SemaphoreType.DMA((slots,)),
                pltpu.SemaphoreType.DMA((slots,)),
                pltpu.SemaphoreType.DMA((2,)),
            ],
            compiler_params=pltpu.CompilerParams(
                collective_id=0, has_side_effects=True, vmem_limit_bytes=32 * 1024 * 1024
            ),
        )(queries, key_value_pairs, span_index, valid_count)

    return jax.shard_map(
        shards,
        mesh=mesh,
        in_specs=(P("span", "seq", None), P("span", "seq", None), P("span"), P("span")),
        out_specs=P("span", "seq", None),
        check_vma=False,
    )
```

```python
import functools
import math

import jax
import jax.numpy as jnp
from jax import lax
from jax.experimental import pallas as pl
from jax.experimental.pallas import tpu as pltpu
from jax.sharding import PartitionSpec as P

MESH = pl.DeviceIdType.MESH
HEAD = 128
LIST = 3
KEYS = 128
META = 16
ROW_EXTRA = 128
SCALE = HEAD ** (-0.5) / math.log(2.0)
NO_MAX = -(2.0**100)
HIDDEN = -(2.0**101)
FAR = 100.0


TREES = (
    {-7: -6, -6: -4, -5: -4, -4: -1, -3: -4, -2: -1, -1: 0, 1: 0, 2: 1, 3: 1, 4: 2, 5: 4, 6: 5, 7: 4, 8: -6},
    {-7: -6, -6: -3, -5: -4, -4: -3, -3: 0, -2: -3, -1: 0, 1: 0, 2: 1, 3: 2, 4: 0, 5: 4, 6: 5, 7: 6, 8: -6},
)
GROUPS = ((0, 1), (-1, 2), (-2, -4), (4, 3), (-3, -6), (-5, 5), (-7, 7), (8, 6))
EVENTS = (
    ((0, 1), (0, -1), (1, 1), (1, -1),),
    ((1, -3),),
    ((1, 4), (0, 2), (0, -2), (1, 2), (0, -4), (0, 3), (1, -2),),
    ((1, -4),),
    ((1, 5), (1, -6),),
    (),
    ((0, 4), (1, 3), (0, -5), (0, -3), (0, -6), (1, 6),),
    ((1, -5),),
    ((1, -7),),
    (),
    ((0, 5), (1, 8),),
    ((0, -7),),
    ((0, 7), (1, 7), (0, 8), (0, 6),),
    (),
    (),
)
CHILDREN = tuple(
    {parent: [child for child in tree if tree[child] == parent] for parent in set(tree.values())} for tree in TREES
)


def hops(child, parent):
    return (child - parent + 8) % 16 - 8


def kernel(
    n_span, n_seq,
    q_hbm, kv_hbm, index_hbm, count_hbm, out_ref,
    kbuf, vbuf, qbuf, place_buf, max_ref, sum_ref, acc_ref, part_buf, got_buf, index_smem, count_smem,
    a2a_send, a2a_recv, ring_send, k_recv, v_recv, int_sem,
):
    tokens = q_hbm.shape[1]
    half_spans = n_span // 2
    n_z = half_spans // 2
    span = lax.axis_index("span")
    seq = lax.axis_index("seq")
    half = lax.div(span, half_spans)
    slot = lax.rem(span, half_spans)
    z = lax.div(slot, 2)
    core = lax.rem(slot, 2)
    group = seq ^ half
    partner_span = (1 - half) * half_spans + slot
    sibling = (half * half_spans + z * 2 + (1 - core), seq)

    def z_at(offset):
        return lax.rem(z + offset + n_z, n_z)

    def along(offset):
        return (half * half_spans + z_at(offset) * 2 + core, seq)

    barrier = pltpu.get_barrier_semaphore()
    for d in range(1, n_seq):
        pl.semaphore_signal(barrier, inc=1, device_id=(span, seq ^ d), device_id_type=MESH)
    for d in range(n_seq):
        pl.semaphore_signal(barrier, inc=1, device_id=(partner_span, seq ^ d), device_id_type=MESH)
    steps = sorted({abs(hops(child, parent)) for tree in TREES for child, parent in tree.items()})
    for s in steps:
        for device in (along(s), along(-s)):
            pl.semaphore_signal(barrier, inc=1, device_id=device, device_id_type=MESH)
    pl.semaphore_signal(barrier, inc=1, device_id=sibling, device_id_type=MESH)

    ints = [
        pltpu.make_async_copy(index_hbm, index_smem, int_sem.at[0]),
        pltpu.make_async_copy(count_hbm, count_smem, int_sem.at[1]),
    ]
    for copy in ints:
        copy.start()
    max_ref[...] = jnp.full(max_ref.shape, NO_MAX, jnp.float32)
    sum_ref[...] = jnp.zeros(sum_ref.shape, jnp.float32)
    acc_ref[...] = jnp.zeros(acc_ref.shape, jnp.float32)
    for copy in ints:
        copy.wait()
    index = index_smem[0].astype(jnp.float32)
    lane = lax.broadcasted_iota(jnp.int32, (META, 128), 1)
    kbuf[slot, KEYS:, :] = jnp.where(lane < count_smem[0], index, FAR).astype(jnp.bfloat16)
    place_buf[0] = jnp.full((META, 128), index, jnp.float32).astype(jnp.bfloat16)

    pl.semaphore_wait(barrier, 2 * n_seq + 2 * len(steps))

    def send(src, dst, send_sem, recv_sem, device):
        pltpu.make_async_remote_copy(
            src_ref=src, dst_ref=dst, send_sem=send_sem, recv_sem=recv_sem, device_id=device, device_id_type=MESH
        ).start()

    def wait(ref, sem):
        pltpu.make_async_copy(ref, ref, sem).wait()

    rows = pl.ds(pl.multiple_of(seq * tokens, tokens), tokens)

    def columns(start, size):
        return pl.ds(pl.multiple_of(start, 128), size)

    for part, buf in ((0, kbuf), (1, vbuf)):
        for d in range(n_seq):
            their = (seq ^ d) ^ half
            src = kv_hbm.at[0, :, columns(their * 256 + part * 128, 128)]
            dst = buf.at[slot, rows, :]
            if d == 0:
                pltpu.make_async_copy(src, dst, a2a_recv.at[part]).start()
            else:
                send(src, dst, a2a_send.at[part], a2a_recv.at[part], (span, seq ^ d))

    for d in range(n_seq):
        their = (seq ^ d) ^ half
        src = q_hbm.at[0, :, columns(their * (LIST * HEAD), LIST * HEAD)]
        dst = qbuf.at[0, rows, :]
        if d == 0:
            pltpu.make_async_copy(src, dst, a2a_recv.at[2]).start()
        else:
            send(src, dst, a2a_send.at[2], a2a_recv.at[2], (span, seq ^ d))
    for d in range(n_seq):
        their = (seq ^ d) ^ (1 - half)
        src = q_hbm.at[0, :, columns(their * (LIST * HEAD), LIST * HEAD)]
        send(src, qbuf.at[1, rows, :], a2a_send.at[3], a2a_recv.at[3], (partner_span, seq ^ d))

    send(place_buf.at[0], place_buf.at[1], a2a_send.at[4], a2a_recv.at[4], (partner_span, seq ^ 1))

    bufs, recvs = (kbuf, vbuf), (k_recv, v_recv)

    def pass_on(chunk, which, device):
        send(bufs[chunk].at[which], bufs[chunk].at[which], ring_send.at[chunk], recvs[chunk].at[which], device)

    def wait_for(chunk, which):
        wait(bufs[chunk].at[which], recvs[chunk].at[which])

    def hand_on(chunk, offset):
        which = z_at(-offset) * 2 + core
        for child in CHILDREN[chunk].get(offset, ()):
            pass_on(chunk, which, along(hops(child, offset)))
        pass_on(chunk, which, sibling)

    wait(kbuf.at[slot, pl.ds(0, KEYS), :], a2a_recv.at[0])
    hand_on(0, 0)
    wait(vbuf.at[slot], a2a_recv.at[1])
    hand_on(1, 0)
    wait(qbuf.at[0], a2a_recv.at[2])
    wait(qbuf.at[1], a2a_recv.at[3])
    wait(place_buf.at[1], a2a_recv.at[4])

    def attend(b, places):
        mine = place_buf[b].astype(jnp.float32)[:1]
        pairs = [pl.ds(place * 2, 2) for place in places]
        metas = [kbuf[pair, KEYS:, :].astype(jnp.float32) for pair in pairs]
        biases = [jnp.where(meta[i, :1] <= mine, 0.0, HIDDEN) for meta in metas for i in range(2)]
        products = []
        for head in range(LIST):
            query = qbuf[b, :, head * HEAD : (head + 1) * HEAD]
            for pair in pairs:
                keys = kbuf[pair, :KEYS, :].reshape(2 * KEYS, HEAD)
                products.append(
                    lax.dot_general(query, keys, (((1,), (1,)), ((), ())), preferred_element_type=jnp.float32)
                )
        weights = []
        for head in range(LIST):
            tile = b * LIST + head
            scores = []
            for i, bias in enumerate(biases):
                product = products[head * len(pairs) + i // 2]
                scores.append(product[:, i % 2 * KEYS : (i % 2 + 1) * KEYS] * SCALE + bias)
            old_max = max_ref[tile]
            top = functools.reduce(jnp.maximum, scores)
            new_max = jnp.maximum(old_max, jnp.max(top, axis=-1, keepdims=True))
            alpha = jnp.exp2(old_max - new_max)
            raw = [jnp.exp2(score - new_max) for score in scores]
            max_ref[tile] = new_max
            sum_ref[tile] = sum_ref[tile] * alpha + functools.reduce(jnp.add, raw)
            weights.append((alpha, [w.astype(jnp.bfloat16) for w in raw]))
        for head in range(LIST):
            tile = b * LIST + head
            alpha, raw = weights[head]
            total = acc_ref[tile] * alpha
            for i, pair in enumerate(pairs):
                values = vbuf[pair].reshape(2 * KEYS, HEAD)
                total += jnp.dot(
                    jnp.concatenate(raw[2 * i : 2 * i + 2], axis=1), values, preferred_element_type=jnp.float32
                )
            acc_ref[tile] = total

    def finish(b):
        lane = lax.broadcasted_iota(jnp.int32, (KEYS, 128), 1)
        stats = jnp.zeros((KEYS, 128), jnp.float32)
        for head in range(LIST):
            tile = b * LIST + head
            top = max_ref[tile]
            sent_max = top.astype(jnp.bfloat16).astype(jnp.float32)
            factor = jnp.exp2(top - sent_max)
            total = jnp.sum(sum_ref[tile], axis=-1, keepdims=True) * factor
            high = total.astype(jnp.bfloat16).astype(jnp.float32)
            stats = jnp.where(lane == 3 * head, sent_max, stats)
            stats = jnp.where(lane == 3 * head + 1, high, stats)
            stats = jnp.where(lane == 3 * head + 2, total - high, stats)
            part_buf[b, :, head * HEAD : (head + 1) * HEAD] = (acc_ref[tile] * factor).astype(jnp.bfloat16)
        part_buf[b, :, LIST * HEAD :] = stats.astype(jnp.bfloat16)
        for d in range(n_seq):
            to = seq ^ d
            src = part_buf.at[b, pl.ds(pl.multiple_of(to * tokens, tokens), tokens), :]
            dst = got_buf.at[b, group]
            if b == 0 and d == 0:
                pltpu.make_async_copy(src, dst, a2a_recv.at[5]).start()
            else:
                device = (span if b == 0 else partner_span, to)
                send(src, dst, a2a_send.at[5 + b], a2a_recv.at[5 + b], device)

    def places_of(g):
        places = []
        for which in range(2):
            offset = GROUPS[0][which]
            for i in range(1, len(GROUPS)):
                offset = jnp.where(g == i, GROUPS[i][which], offset)
            places.append(z_at(-offset))
        return places

    def loop(i, carry):
        for at, events in enumerate(EVENTS):
            if events:

                @pl.when(i == at)
                def _():
                    for chunk, offset in events:
                        wait_for(chunk, z_at(-offset) * 2 + core)
                        hand_on(chunk, offset)

        places = places_of(lax.div(i, 2))

        @pl.when(lax.rem(i, 2) == 0)
        def _():
            for place in places:
                for chunk in range(2):
                    wait_for(chunk, place * 2 + 1 - core)

        attend(1 - lax.rem(i, 2), places)
        return carry

    lax.fori_loop(0, 2 * len(GROUPS) - 1, loop, 0)
    finish(1)
    attend(0, [z_at(-offset) for offset in GROUPS[-1]])
    finish(0)

    wait(kbuf.at[pl.ds(0, half_spans - 1)], ring_send.at[0])
    wait(vbuf.at[pl.ds(0, half_spans - 1)], ring_send.at[1])
    wait(vbuf.at[0, pl.ds(0, (n_seq - 1) * tokens), :], a2a_send.at[0])
    wait(vbuf.at[0, pl.ds(0, (n_seq - 1) * tokens), :], a2a_send.at[1])
    wait(qbuf.at[0, pl.ds(0, (n_seq - 1) * tokens), :], a2a_send.at[2])
    wait(qbuf.at[1], a2a_send.at[3])
    wait(place_buf.at[0], a2a_send.at[4])

    wait(got_buf.at[1], a2a_recv.at[6])
    wait(got_buf.at[0], a2a_recv.at[5])
    for g in range(n_seq):
        stats = [got_buf[b, g, :, LIST * HEAD :].astype(jnp.float32) for b in range(2)]
        for head in range(LIST):
            tops = [s[:, 3 * head : 3 * head + 1] for s in stats]
            totals = [s[:, 3 * head + 1 : 3 * head + 2] + s[:, 3 * head + 2 : 3 * head + 3] for s in stats]
            top = jnp.maximum(*tops)
            shares = [jnp.exp2(t - top) for t in tops]
            whole = shares[0] * totals[0] + shares[1] * totals[1]
            shares = [s / whole for s in shares]
            parts = [got_buf[b, g, :, head * HEAD : (head + 1) * HEAD].astype(jnp.float32) for b in range(2)]
            place = (g * LIST + head) * HEAD
            out_ref[0, :, place : place + HEAD] = (parts[0] * shares[0] + parts[1] * shares[1]).astype(jnp.bfloat16)
    wait(part_buf.at[0, pl.ds(0, (n_seq - 1) * tokens), :], a2a_send.at[5])
    wait(part_buf.at[1], a2a_send.at[6])


def solution(mesh):
    n_span, n_seq = mesh.shape["span"], mesh.shape["seq"]
    slots = n_span // 2

    def shards(queries, key_value_pairs, span_index, valid_count):
        tokens = queries.shape[1]
        return pl.pallas_call(
            functools.partial(kernel, n_span, n_seq),
            out_shape=jax.ShapeDtypeStruct(queries.shape, jnp.bfloat16),
            in_specs=[pl.BlockSpec(memory_space=pl.ANY)] * 4,
            out_specs=pl.BlockSpec(memory_space=pltpu.VMEM),
            scratch_shapes=[
                pltpu.VMEM((slots, KEYS + META, HEAD), jnp.bfloat16),
                pltpu.VMEM((slots, KEYS, HEAD), jnp.bfloat16),
                pltpu.VMEM((2, KEYS, LIST * HEAD), jnp.bfloat16),
                pltpu.VMEM((2, META, 128), jnp.bfloat16),
                pltpu.VMEM((2 * LIST, KEYS, HEAD), jnp.float32),
                pltpu.VMEM((2 * LIST, KEYS, HEAD), jnp.float32),
                pltpu.VMEM((2 * LIST, KEYS, HEAD), jnp.float32),
                pltpu.VMEM((2, KEYS, LIST * HEAD + ROW_EXTRA), jnp.bfloat16),
                pltpu.VMEM((2, n_seq, tokens, LIST * HEAD + ROW_EXTRA), jnp.bfloat16),
                pltpu.SMEM((1,), jnp.int32),
                pltpu.SMEM((1,), jnp.int32),
                pltpu.SemaphoreType.DMA((7,)),
                pltpu.SemaphoreType.DMA((7,)),
                pltpu.SemaphoreType.DMA((2,)),
                pltpu.SemaphoreType.DMA((slots,)),
                pltpu.SemaphoreType.DMA((slots,)),
                pltpu.SemaphoreType.DMA((2,)),
            ],
            compiler_params=pltpu.CompilerParams(
                collective_id=0, has_side_effects=True, vmem_limit_bytes=60 * 1024 * 1024
            ),
        )(queries, key_value_pairs, span_index, valid_count)

    return jax.shard_map(
        shards,
        mesh=mesh,
        in_specs=(P("span", "seq", None), P("span", "seq", None), P("span"), P("span")),
        out_specs=P("span", "seq", None),
        check_vma=False,
    )
```

```python
import functools
import math

import jax
import jax.numpy as jnp
from jax import lax
from jax.experimental import pallas as pl
from jax.experimental.pallas import tpu as pltpu
from jax.sharding import PartitionSpec as P

MESH = pl.DeviceIdType.MESH
HEAD = 128
LIST = 3
KEYS = 128
META = 16
ROW_EXTRA = 128
SCALE = HEAD ** (-0.5) / math.log(2.0)
NO_MAX = -(2.0**100)
HIDDEN = -(2.0**101)
FAR = 100.0


TREES = (
    {-7: -6, -6: -4, -5: -4, -4: -3, -3: -2, -2: -1, -1: 0, 1: 0, 2: 1, 3: 2, 4: 3, 5: 3, 6: 5, 7: 4, 8: 7},
    {-7: -6, -6: -3, -5: -4, -4: -3, -3: -2, -2: 0, -1: 0, 1: 0, 2: 1, 3: 4, 4: 0, 5: 4, 6: 5, 7: 5, 8: -6},
)
DIRECT = (3, -3)
GROUPS = ((0, -1), (1, 3), (-3, -2), (4, -4), (2, 5), (-6, -5), (6, 7), (-7, 8))
EVENTS = (
    ((0, -1), (0, 1), (0, 3), (0, -3), (1, -1), (1, 1), (1, 3), (1, -3), (1, -2),),
    (),
    ((0, -2),),
    ((1, 4),),
    ((0, -4), (0, 2), (0, 4),),
    (),
    ((1, -4), (1, 2), (0, 5),),
    ((1, -6), (1, 5),),
    ((0, -5),),
    ((0, -6),),
    ((0, 7), (1, -5), (0, 6), (1, -7), (1, 6),),
    (),
    ((1, 8), (1, 7), (0, -7), (0, 8),),
    (),
    (),
)
CHILDREN = tuple(
    {parent: [child for child in tree if tree[child] == parent and child not in DIRECT] for parent in set(tree.values())} for tree in TREES
)


def hops(child, parent):
    return (child - parent + 8) % 16 - 8


def kernel(
    n_span, n_seq,
    q_hbm, kv_hbm, index_ref, count_ref, out_ref,
    kbuf, vbuf, qbuf, place_buf, max_ref, sum_ref, acc_ref, part_buf, got_buf,
    a2a_send, a2a_recv, ring_send, k_recv, v_recv,
):
    tokens = q_hbm.shape[1]
    half_spans = n_span // 2
    n_z = half_spans // 2
    span = lax.axis_index("span")
    seq = lax.axis_index("seq")
    half = lax.div(span, half_spans)
    slot = lax.rem(span, half_spans)
    z = lax.div(slot, 2)
    core = lax.rem(slot, 2)
    group = seq ^ half
    partner_span = (1 - half) * half_spans + slot
    sibling = (half * half_spans + z * 2 + (1 - core), seq)

    def z_at(offset):
        return lax.rem(z + offset + n_z, n_z)

    def along(offset):
        return (half * half_spans + z_at(offset) * 2 + core, seq)

    barrier = pltpu.get_barrier_semaphore()
    peers = [(span, seq ^ d) for d in range(1, n_seq)]
    peers += [(partner_span, seq ^ d) for d in range(n_seq)]
    steps = sorted({child - parent for tree in TREES for child, parent in tree.items()} | {abs(n) for n in DIRECT})
    steps = [s for s in steps if s > 0]
    peers += [along(sign * s) for s in steps for sign in (1, -1)]
    peers += [(along(n)[0], seq ^ d) for n in DIRECT for d in range(1, n_seq)]
    peers.append(sibling)
    for device in peers:
        pl.semaphore_signal(barrier, inc=1, device_id=device, device_id_type=MESH)

    max_ref[...] = jnp.full(max_ref.shape, NO_MAX, jnp.float32)
    sum_ref[...] = jnp.zeros(sum_ref.shape, jnp.float32)
    acc_ref[...] = jnp.zeros(acc_ref.shape, jnp.float32)
    index = index_ref[0].astype(jnp.float32)
    lane = lax.broadcasted_iota(jnp.int32, (META, 128), 1)
    kbuf[slot, KEYS:, :] = jnp.where(lane < count_ref[0], index, FAR).astype(jnp.bfloat16)
    place_buf[0] = jnp.full((META, 128), index, jnp.float32).astype(jnp.bfloat16)

    pl.semaphore_wait(barrier, len(peers))

    def send(src, dst, send_sem, recv_sem, device):
        pltpu.make_async_remote_copy(
            src_ref=src, dst_ref=dst, send_sem=send_sem, recv_sem=recv_sem, device_id=device, device_id_type=MESH
        ).start()

    def wait(ref, sem):
        pltpu.make_async_copy(ref, ref, sem).wait()

    rows = pl.ds(pl.multiple_of(seq * tokens, tokens), tokens)

    def columns(start, size):
        return pl.ds(pl.multiple_of(start, 128), size)

    meta = kbuf.at[slot, pl.ds(KEYS, META), :]
    for n in DIRECT:
        send(meta, meta, a2a_send.at[7], k_recv.at[slot], along(n))
    for part, buf, recv in ((0, kbuf, k_recv), (1, vbuf, v_recv)):
        for n in (*DIRECT, 0):
            for d in range(n_seq):
                their = (seq ^ d) ^ half
                src = kv_hbm.at[0, :, columns(their * 256 + part * 128, 128)]
                dst = buf.at[slot, rows, :]
                if n:
                    send(src, dst, a2a_send.at[8 + part], recv.at[slot], (along(n)[0], seq ^ d))
                elif d:
                    send(src, dst, a2a_send.at[part], a2a_recv.at[part], (span, seq ^ d))
                else:
                    pltpu.make_async_copy(src, dst, a2a_recv.at[part]).start()

    for d in range(n_seq):
        their = (seq ^ d) ^ half
        src = q_hbm.at[0, :, columns(their * (LIST * HEAD), LIST * HEAD)]
        dst = qbuf.at[0, rows, :]
        if d == 0:
            pltpu.make_async_copy(src, dst, a2a_recv.at[2]).start()
        else:
            send(src, dst, a2a_send.at[2], a2a_recv.at[2], (span, seq ^ d))
    for d in range(n_seq):
        their = (seq ^ d) ^ (1 - half)
        src = q_hbm.at[0, :, columns(their * (LIST * HEAD), LIST * HEAD)]
        send(src, qbuf.at[1, rows, :], a2a_send.at[3], a2a_recv.at[3], (partner_span, seq ^ d))

    send(place_buf.at[0], place_buf.at[1], a2a_send.at[4], a2a_recv.at[4], (partner_span, seq ^ 1))

    bufs, recvs = (kbuf, vbuf), (k_recv, v_recv)

    def pass_on(chunk, which, device):
        send(bufs[chunk].at[which], bufs[chunk].at[which], ring_send.at[chunk], recvs[chunk].at[which], device)

    def wait_for(chunk, which):
        wait(bufs[chunk].at[which], recvs[chunk].at[which])

    def hand_on(chunk, offset):
        which = z_at(-offset) * 2 + core
        for child in CHILDREN[chunk].get(offset, ()):
            pass_on(chunk, which, along(hops(child, offset)))
        pass_on(chunk, which, sibling)

    wait(kbuf.at[slot, pl.ds(0, KEYS), :], a2a_recv.at[0])
    hand_on(0, 0)
    wait(vbuf.at[slot], a2a_recv.at[1])
    hand_on(1, 0)

    def attend(b, pairs):
        mine = place_buf[b].astype(jnp.float32)[:1]
        metas = [kbuf[which, KEYS:, :].astype(jnp.float32) for pair in pairs for which in pair]
        biases = [jnp.where(meta[:1] <= mine, 0.0, HIDDEN) for meta in metas]
        products = []
        for head in range(LIST):
            query = qbuf[b, :, head * HEAD : (head + 1) * HEAD]
            for pair in pairs:
                keys = jnp.concatenate([kbuf[which, :KEYS, :] for which in pair], axis=0)
                products.append(
                    lax.dot_general(query, keys, (((1,), (1,)), ((), ())), preferred_element_type=jnp.float32)
                )
        weights = []
        for head in range(LIST):
            tile = b * LIST + head
            scores = []
            for i, bias in enumerate(biases):
                product = products[head * len(pairs) + i // 2]
                scores.append(product[:, i % 2 * KEYS : (i % 2 + 1) * KEYS] * SCALE + bias)
            old_max = max_ref[tile]
            top = functools.reduce(jnp.maximum, scores)
            new_max = jnp.maximum(old_max, jnp.max(top, axis=-1, keepdims=True))
            alpha = jnp.exp2(old_max - new_max)
            raw = [jnp.exp2(score - new_max) for score in scores]
            max_ref[tile] = new_max
            sum_ref[tile] = sum_ref[tile] * alpha + functools.reduce(jnp.add, raw)
            weights.append((alpha, [w.astype(jnp.bfloat16) for w in raw]))
        for head in range(LIST):
            tile = b * LIST + head
            alpha, raw = weights[head]
            total = acc_ref[tile] * alpha
            for i, pair in enumerate(pairs):
                values = jnp.concatenate([vbuf[which] for which in pair], axis=0)
                total += jnp.dot(
                    jnp.concatenate(raw[2 * i : 2 * i + 2], axis=1), values, preferred_element_type=jnp.float32
                )
            acc_ref[tile] = total

    def finish(b):
        lane = lax.broadcasted_iota(jnp.int32, (KEYS, 128), 1)
        stats = jnp.zeros((KEYS, 128), jnp.float32)
        for head in range(LIST):
            tile = b * LIST + head
            top = max_ref[tile]
            sent_max = top.astype(jnp.bfloat16).astype(jnp.float32)
            factor = jnp.exp2(top - sent_max)
            total = jnp.sum(sum_ref[tile], axis=-1, keepdims=True) * factor
            high = total.astype(jnp.bfloat16).astype(jnp.float32)
            stats = jnp.where(lane == 3 * head, sent_max, stats)
            stats = jnp.where(lane == 3 * head + 1, high, stats)
            stats = jnp.where(lane == 3 * head + 2, total - high, stats)
            part_buf[b, :, head * HEAD : (head + 1) * HEAD] = (acc_ref[tile] * factor).astype(jnp.bfloat16)
        part_buf[b, :, LIST * HEAD :] = stats.astype(jnp.bfloat16)
        for d in range(n_seq):
            to = seq ^ d
            src = part_buf.at[b, pl.ds(pl.multiple_of(to * tokens, tokens), tokens), :]
            dst = got_buf.at[b, group]
            if b == 0 and d == 0:
                pltpu.make_async_copy(src, dst, a2a_recv.at[5]).start()
            else:
                device = (span if b == 0 else partner_span, to)
                send(src, dst, a2a_send.at[5 + b], a2a_recv.at[5 + b], device)

    def places_of(g):
        places = []
        for which in range(2):
            offset = GROUPS[0][which]
            for i in range(1, len(GROUPS)):
                offset = jnp.where(g == i, GROUPS[i][which], offset)
            places.append(z_at(-offset))
        return places

    def arrive(events):
        for chunk, offset in events:
            wait_for(chunk, z_at(-offset) * 2 + core)
            hand_on(chunk, offset)

    def wait_other(places):
        for place in places:
            for chunk in range(2):
                wait_for(chunk, place * 2 + 1 - core)

    def loop(i, carry):
        for at, events in enumerate(EVENTS[:-1]):
            if events:

                @pl.when(i == at)
                def _():
                    arrive(events)

        @pl.when(i == 0)
        def _():
            wait(qbuf.at[0], a2a_recv.at[2])
            wait(qbuf.at[1], a2a_recv.at[3])
            wait(place_buf.at[1], a2a_recv.at[4])

        places = places_of(lax.div(i, 2))

        @pl.when(lax.rem(i, 2) == 0)
        def _():
            wait_other(places)

        attend(1 - lax.rem(i, 2), [[place * 2, place * 2 + 1] for place in places])
        return carry

    lax.fori_loop(0, len(EVENTS) - 1, loop, 0)
    arrive(EVENTS[-1])
    places = [z_at(-offset) for offset in GROUPS[-1]]
    own = [[place * 2 + core for place in places]]
    others = [[place * 2 + 1 - core for place in places]]
    attend(1, own)
    attend(0, own)
    wait_other(places)
    attend(1, others)
    finish(1)
    attend(0, others)
    finish(0)

    wait(kbuf.at[pl.ds(0, half_spans - 1 - len(DIRECT))], ring_send.at[0])
    wait(vbuf.at[pl.ds(0, half_spans - 1 - len(DIRECT))], ring_send.at[1])
    if DIRECT:
        wait(place_buf.at[pl.ds(0, len(DIRECT))], a2a_send.at[7])
        wait(vbuf.at[pl.ds(0, len(DIRECT))], a2a_send.at[8])
        wait(vbuf.at[pl.ds(0, len(DIRECT))], a2a_send.at[9])
    wait(vbuf.at[0, pl.ds(0, (n_seq - 1) * tokens), :], a2a_send.at[0])
    wait(vbuf.at[0, pl.ds(0, (n_seq - 1) * tokens), :], a2a_send.at[1])
    wait(qbuf.at[0, pl.ds(0, (n_seq - 1) * tokens), :], a2a_send.at[2])
    wait(qbuf.at[1], a2a_send.at[3])
    wait(place_buf.at[0], a2a_send.at[4])

    wait(got_buf.at[1], a2a_recv.at[6])
    wait(got_buf.at[0], a2a_recv.at[5])
    for g in range(n_seq):
        stats = [got_buf[b, g, :, LIST * HEAD :].astype(jnp.float32) for b in range(2)]
        for head in range(LIST):
            tops = [s[:, 3 * head : 3 * head + 1] for s in stats]
            totals = [s[:, 3 * head + 1 : 3 * head + 2] + s[:, 3 * head + 2 : 3 * head + 3] for s in stats]
            top = jnp.maximum(*tops)
            shares = [jnp.exp2(t - top) for t in tops]
            whole = shares[0] * totals[0] + shares[1] * totals[1]
            shares = [s / whole for s in shares]
            parts = [got_buf[b, g, :, head * HEAD : (head + 1) * HEAD].astype(jnp.float32) for b in range(2)]
            place = (g * LIST + head) * HEAD
            out_ref[0, :, place : place + HEAD] = (parts[0] * shares[0] + parts[1] * shares[1]).astype(jnp.bfloat16)
    wait(part_buf.at[0, pl.ds(0, (n_seq - 1) * tokens), :], a2a_send.at[5])
    wait(part_buf.at[1], a2a_send.at[6])


def solution(mesh):
    n_span, n_seq = mesh.shape["span"], mesh.shape["seq"]
    slots = n_span // 2

    def shards(queries, key_value_pairs, span_index, valid_count):
        tokens = queries.shape[1]
        return pl.pallas_call(
            functools.partial(kernel, n_span, n_seq),
            out_shape=jax.ShapeDtypeStruct(queries.shape, jnp.bfloat16),
            in_specs=[pl.BlockSpec(memory_space=pl.ANY)] * 2 + [pl.BlockSpec(memory_space=pltpu.SMEM)] * 2,
            out_specs=pl.BlockSpec(memory_space=pltpu.VMEM),
            scratch_shapes=[
                pltpu.VMEM((slots, KEYS + META, HEAD), jnp.bfloat16),
                pltpu.VMEM((slots, KEYS, HEAD), jnp.bfloat16),
                pltpu.VMEM((2, KEYS, LIST * HEAD), jnp.bfloat16),
                pltpu.VMEM((8, META, 128), jnp.bfloat16),
                pltpu.VMEM((2 * LIST, KEYS, HEAD), jnp.float32),
                pltpu.VMEM((2 * LIST, KEYS, HEAD), jnp.float32),
                pltpu.VMEM((2 * LIST, KEYS, HEAD), jnp.float32),
                pltpu.VMEM((2, KEYS, LIST * HEAD + ROW_EXTRA), jnp.bfloat16),
                pltpu.VMEM((2, n_seq, tokens, LIST * HEAD + ROW_EXTRA), jnp.bfloat16),
                pltpu.SemaphoreType.DMA((10,)),
                pltpu.SemaphoreType.DMA((7,)),
                pltpu.SemaphoreType.DMA((2,)),
                pltpu.SemaphoreType.DMA((slots,)),
                pltpu.SemaphoreType.DMA((slots,)),
            ],
            compiler_params=pltpu.CompilerParams(
                collective_id=0, has_side_effects=True, vmem_limit_bytes=32 * 1024 * 1024
            ),
        )(
            pltpu.with_memory_space_constraint(queries, pltpu.HBM),
            pltpu.with_memory_space_constraint(key_value_pairs, pltpu.HBM),
            span_index,
            valid_count,
        )

    return jax.shard_map(
        shards,
        mesh=mesh,
        in_specs=(P("span", "seq", None), P("span", "seq", None), P("span"), P("span")),
        out_specs=P("span", "seq", None),
        check_vma=False,
    )
```

```python
import functools
import math

import jax
import jax.numpy as jnp
from jax import lax
from jax.experimental import pallas as pl
from jax.experimental.pallas import tpu as pltpu
from jax.sharding import PartitionSpec as P

MESH = pl.DeviceIdType.MESH
HEAD = 128
LIST = 3
KEYS = 128
HALF = KEYS // 2
META = 16
ROW_EXTRA = 128
SCALE = HEAD ** (-0.5) / math.log(2.0)
NO_MAX = -(2.0**100)
HIDDEN = -(2.0**101)
FAR = 100.0


TREES = (
    {-7: -6, -6: -4, -5: -4, -4: -3, -3: -2, -2: -1, -1: 0, 1: 0, 2: 1, 3: 2, 4: 3, 5: 3, 6: 5, 7: 4, 8: 7},
    {-7: -6, -6: -3, -5: -4, -4: -3, -3: -2, -2: 0, -1: 0, 1: 0, 2: 1, 3: 4, 4: 0, 5: 4, 6: 5, 7: 5, 8: -6},
)
DIRECT = (3, -3)
GROUPS = ((0, -1), (1, 3), (-3, -2), (4, -4), (2, 5), (-6, -5), (6, 7), (-7, 8))
EVENTS = (
    ((0, -1), (0, 1), (0, 3), (0, -3), (1, -1), (1, 1), (1, 3), (1, -3), (1, -2),),
    (),
    ((0, -2),),
    ((1, 4),),
    ((0, -4), (0, 2), (0, 4),),
    (),
    ((1, -4), (1, 2), (0, 5),),
    ((1, -6), (1, 5),),
    ((0, -5),),
    ((0, -6),),
    ((0, 7), (1, -5), (0, 6), (1, -7), (1, 6),),
    (),
    ((1, 8), (1, 7), (0, -7), (0, 8),),
    (),
    (),
)
CHILDREN = tuple(
    {parent: [child for child in tree if tree[child] == parent and child not in DIRECT] for parent in set(tree.values())} for tree in TREES
)


def hops(child, parent):
    return (child - parent + 8) % 16 - 8


def kernel(
    n_span, n_seq,
    q_hbm, kv_hbm, index_ref, count_ref, out_ref,
    kvbuf, metabuf, qbuf, place_buf, max_ref, sum_ref, acc_ref, part_buf, got_buf,
    a2a_send, a2a_recv, ring_send, chunk_recv, meta_recv,
):
    tokens = q_hbm.shape[1]
    half_spans = n_span // 2
    n_z = half_spans // 2
    span = lax.axis_index("span")
    seq = lax.axis_index("seq")
    half = lax.div(span, half_spans)
    slot = lax.rem(span, half_spans)
    z = lax.div(slot, 2)
    core = lax.rem(slot, 2)
    group = seq ^ half
    partner_span = (1 - half) * half_spans + slot
    sibling = (half * half_spans + z * 2 + (1 - core), seq)

    def z_at(offset):
        return lax.rem(z + offset + n_z, n_z)

    def along(offset):
        return (half * half_spans + z_at(offset) * 2 + core, seq)

    barrier = pltpu.get_barrier_semaphore()
    peers = [(span, seq ^ d) for d in range(1, n_seq)]
    peers += [(partner_span, seq ^ d) for d in range(n_seq)]
    steps = sorted({child - parent for tree in TREES for child, parent in tree.items()} | {abs(n) for n in DIRECT})
    steps = [s for s in steps if s > 0]
    peers += [along(sign * s) for s in steps for sign in (1, -1)]
    peers += [(along(n)[0], seq ^ d) for n in DIRECT for d in range(1, n_seq)]
    peers.append(sibling)
    for device in peers:
        pl.semaphore_signal(barrier, inc=1, device_id=device, device_id_type=MESH)

    max_ref[...] = jnp.full(max_ref.shape, NO_MAX, jnp.float32)
    sum_ref[...] = jnp.zeros(sum_ref.shape, jnp.float32)
    acc_ref[...] = jnp.zeros(acc_ref.shape, jnp.float32)
    index = index_ref[0].astype(jnp.float32)
    lane = lax.broadcasted_iota(jnp.int32, (1, 128), 1)
    metabuf[slot] = jnp.where(lane < count_ref[0], index, FAR)
    place_buf[0] = jnp.full((META, 128), index, jnp.float32).astype(jnp.bfloat16)

    pl.semaphore_wait(barrier, len(peers))

    def send(src, dst, send_sem, recv_sem, device):
        pltpu.make_async_remote_copy(
            src_ref=src, dst_ref=dst, send_sem=send_sem, recv_sem=recv_sem, device_id=device, device_id_type=MESH
        ).start()

    def wait(ref, sem):
        pltpu.make_async_copy(ref, ref, sem).wait()

    rows = pl.ds(pl.multiple_of(seq * tokens, tokens), tokens)

    def columns(start, size):
        return pl.ds(pl.multiple_of(start, 128), size)

    for n in DIRECT:
        send(metabuf.at[slot], metabuf.at[slot], ring_send.at[2], meta_recv.at[slot], along(n))
    own_chunk = lax.div(seq, n_seq // 2)
    for n in (0, *DIRECT):
        for d in range(n_seq):
            their = (seq ^ d) ^ half
            src = kv_hbm.at[0, :, columns(their * 256, 256)]
            dst = kvbuf.at[slot, rows, :]
            if n:
                send(src, dst, a2a_send.at[1], chunk_recv.at[own_chunk, slot], (along(n)[0], seq ^ d))
            elif d:
                send(src, dst, a2a_send.at[0], a2a_recv.at[own_chunk], (span, seq ^ d))
            else:
                pltpu.make_async_copy(src, dst, a2a_recv.at[own_chunk]).start()

    for d in range(n_seq):
        their = (seq ^ d) ^ half
        src = q_hbm.at[0, :, columns(their * (LIST * HEAD), LIST * HEAD)]
        dst = qbuf.at[0, rows, :]
        if d == 0:
            pltpu.make_async_copy(src, dst, a2a_recv.at[2]).start()
        else:
            send(src, dst, a2a_send.at[2], a2a_recv.at[2], (span, seq ^ d))
    for d in range(n_seq):
        their = (seq ^ d) ^ (1 - half)
        src = q_hbm.at[0, :, columns(their * (LIST * HEAD), LIST * HEAD)]
        send(src, qbuf.at[1, rows, :], a2a_send.at[3], a2a_recv.at[3], (partner_span, seq ^ d))

    send(place_buf.at[0], place_buf.at[1], a2a_send.at[4], a2a_recv.at[4], (partner_span, seq ^ 1))

    def chunk_of(chunk, which):
        return kvbuf.at[which, pl.ds(chunk * HALF, HALF), :]

    def pass_on(chunk, which, device):
        ref = chunk_of(chunk, which)
        send(ref, ref, ring_send.at[chunk], chunk_recv.at[chunk, which], device)
        if chunk == 0:
            send(metabuf.at[which], metabuf.at[which], ring_send.at[2], meta_recv.at[which], device)

    def wait_for(chunk, which):
        if chunk == 0:
            wait(metabuf.at[which], meta_recv.at[which])
        wait(chunk_of(chunk, which), chunk_recv.at[chunk, which])

    def hand_on(chunk, offset):
        which = z_at(-offset) * 2 + core
        for child in CHILDREN[chunk].get(offset, ()):
            pass_on(chunk, which, along(hops(child, offset)))
        pass_on(chunk, which, sibling)

    for chunk in range(2):
        wait(chunk_of(chunk, slot), a2a_recv.at[chunk])
        hand_on(chunk, 0)

    def attend(b, pairs):
        mine = place_buf[b].astype(jnp.float32)[:1]
        metas = [metabuf[which] for pair in pairs for which in pair]
        biases = [jnp.where(meta <= mine, 0.0, HIDDEN) for meta in metas]
        products = []
        for head in range(LIST):
            query = qbuf[b, :, head * HEAD : (head + 1) * HEAD]
            for pair in pairs:
                keys = jnp.concatenate([kvbuf[which, :, :HEAD] for which in pair], axis=0)
                products.append(
                    lax.dot_general(query, keys, (((1,), (1,)), ((), ())), preferred_element_type=jnp.float32)
                )
        weights = []
        for head in range(LIST):
            tile = b * LIST + head
            scores = []
            for i, bias in enumerate(biases):
                product = products[head * len(pairs) + i // 2]
                scores.append(product[:, i % 2 * KEYS : (i % 2 + 1) * KEYS] * SCALE + bias)
            old_max = max_ref[tile]
            top = functools.reduce(jnp.maximum, scores)
            new_max = jnp.maximum(old_max, jnp.max(top, axis=-1, keepdims=True))
            alpha = jnp.exp2(old_max - new_max)
            raw = [jnp.exp2(score - new_max) for score in scores]
            max_ref[tile] = new_max
            sum_ref[tile] = sum_ref[tile] * alpha + functools.reduce(jnp.add, raw)
            weights.append((alpha, [w.astype(jnp.bfloat16) for w in raw]))
        for head in range(LIST):
            tile = b * LIST + head
            alpha, raw = weights[head]
            total = acc_ref[tile] * alpha
            for i, pair in enumerate(pairs):
                values = jnp.concatenate([kvbuf[which, :, HEAD:] for which in pair], axis=0)
                total += jnp.dot(
                    jnp.concatenate(raw[2 * i : 2 * i + 2], axis=1), values, preferred_element_type=jnp.float32
                )
            acc_ref[tile] = total

    def finish(b):
        lane = lax.broadcasted_iota(jnp.int32, (KEYS, 128), 1)
        stats = jnp.zeros((KEYS, 128), jnp.float32)
        for head in range(LIST):
            tile = b * LIST + head
            top = max_ref[tile]
            sent_max = top.astype(jnp.bfloat16).astype(jnp.float32)
            factor = jnp.exp2(top - sent_max)
            total = jnp.sum(sum_ref[tile], axis=-1, keepdims=True) * factor
            high = total.astype(jnp.bfloat16).astype(jnp.float32)
            stats = jnp.where(lane == 3 * head, sent_max, stats)
            stats = jnp.where(lane == 3 * head + 1, high, stats)
            stats = jnp.where(lane == 3 * head + 2, total - high, stats)
            part_buf[b, :, head * HEAD : (head + 1) * HEAD] = (acc_ref[tile] * factor).astype(jnp.bfloat16)
        part_buf[b, :, LIST * HEAD :] = stats.astype(jnp.bfloat16)
        for d in range(n_seq):
            to = seq ^ d
            src = part_buf.at[b, pl.ds(pl.multiple_of(to * tokens, tokens), tokens), :]
            dst = got_buf.at[b, group]
            if b == 0 and d == 0:
                pltpu.make_async_copy(src, dst, a2a_recv.at[5]).start()
            else:
                device = (span if b == 0 else partner_span, to)
                send(src, dst, a2a_send.at[5 + b], a2a_recv.at[5 + b], device)

    def places_of(g):
        places = []
        for which in range(2):
            offset = GROUPS[0][which]
            for i in range(1, len(GROUPS)):
                offset = jnp.where(g == i, GROUPS[i][which], offset)
            places.append(z_at(-offset))
        return places

    def arrive(events):
        for chunk, offset in events:
            wait_for(chunk, z_at(-offset) * 2 + core)
            hand_on(chunk, offset)

    def wait_other(places):
        for place in places:
            for chunk in range(2):
                wait_for(chunk, place * 2 + 1 - core)

    def loop(i, carry):
        for at, events in enumerate(EVENTS[:-1]):
            if events:

                @pl.when(i == at)
                def _():
                    arrive(events)

        @pl.when(i == 0)
        def _():
            wait(qbuf.at[0], a2a_recv.at[2])
            wait(qbuf.at[1], a2a_recv.at[3])
            wait(place_buf.at[1], a2a_recv.at[4])

        places = places_of(lax.div(i, 2))

        @pl.when(lax.rem(i, 2) == 0)
        def _():
            wait_other(places)

        attend(1 - lax.rem(i, 2), [[place * 2, place * 2 + 1] for place in places])
        return carry

    lax.fori_loop(0, len(EVENTS) - 1, loop, 0)
    arrive(EVENTS[-1])
    places = [z_at(-offset) for offset in GROUPS[-1]]
    own = [[place * 2 + core for place in places]]
    others = [[place * 2 + 1 - core for place in places]]
    attend(1, own)
    attend(0, own)
    wait_other(places)
    attend(1, others)
    finish(1)
    attend(0, others)
    finish(0)

    for chunk in range(2):
        wait(kvbuf.at[pl.ds(0, half_spans - 1 - len(DIRECT)), pl.ds(0, HALF), :], ring_send.at[chunk])
    wait(metabuf.at[pl.ds(0, half_spans - 1)], ring_send.at[2])
    wait(kvbuf.at[0, pl.ds(0, (n_seq - 1) * tokens), :], a2a_send.at[0])
    if DIRECT:
        wait(kvbuf.at[pl.ds(0, len(DIRECT))], a2a_send.at[1])
    wait(qbuf.at[0, pl.ds(0, (n_seq - 1) * tokens), :], a2a_send.at[2])
    wait(qbuf.at[1], a2a_send.at[3])
    wait(place_buf.at[0], a2a_send.at[4])

    wait(got_buf.at[1], a2a_recv.at[6])
    wait(got_buf.at[0], a2a_recv.at[5])
    for g in range(n_seq):
        stats = [got_buf[b, g, :, LIST * HEAD :].astype(jnp.float32) for b in range(2)]
        for head in range(LIST):
            tops = [s[:, 3 * head : 3 * head + 1] for s in stats]
            totals = [s[:, 3 * head + 1 : 3 * head + 2] + s[:, 3 * head + 2 : 3 * head + 3] for s in stats]
            top = jnp.maximum(*tops)
            shares = [jnp.exp2(t - top) for t in tops]
            whole = shares[0] * totals[0] + shares[1] * totals[1]
            shares = [s / whole for s in shares]
            parts = [got_buf[b, g, :, head * HEAD : (head + 1) * HEAD].astype(jnp.float32) for b in range(2)]
            place = (g * LIST + head) * HEAD
            out_ref[0, :, place : place + HEAD] = (parts[0] * shares[0] + parts[1] * shares[1]).astype(jnp.bfloat16)
    wait(part_buf.at[0, pl.ds(0, (n_seq - 1) * tokens), :], a2a_send.at[5])
    wait(part_buf.at[1], a2a_send.at[6])


def solution(mesh):
    n_span, n_seq = mesh.shape["span"], mesh.shape["seq"]
    slots = n_span // 2

    def shards(queries, key_value_pairs, span_index, valid_count):
        tokens = queries.shape[1]
        return pl.pallas_call(
            functools.partial(kernel, n_span, n_seq),
            out_shape=jax.ShapeDtypeStruct(queries.shape, jnp.bfloat16),
            in_specs=[pl.BlockSpec(memory_space=pl.ANY)] * 2 + [pl.BlockSpec(memory_space=pltpu.SMEM)] * 2,
            out_specs=pl.BlockSpec(memory_space=pltpu.VMEM),
            scratch_shapes=[
                pltpu.VMEM((slots, KEYS, 2 * HEAD), jnp.bfloat16),
                pltpu.VMEM((slots, 1, 128), jnp.float32),
                pltpu.VMEM((2, KEYS, LIST * HEAD), jnp.bfloat16),
                pltpu.VMEM((2, META, 128), jnp.bfloat16),
                pltpu.VMEM((2 * LIST, KEYS, HEAD), jnp.float32),
                pltpu.VMEM((2 * LIST, KEYS, HEAD), jnp.float32),
                pltpu.VMEM((2 * LIST, KEYS, HEAD), jnp.float32),
                pltpu.VMEM((2, KEYS, LIST * HEAD + ROW_EXTRA), jnp.bfloat16),
                pltpu.VMEM((2, n_seq, tokens, LIST * HEAD + ROW_EXTRA), jnp.bfloat16),
                pltpu.SemaphoreType.DMA((7,)),
                pltpu.SemaphoreType.DMA((7,)),
                pltpu.SemaphoreType.DMA((3,)),
                pltpu.SemaphoreType.DMA((2, slots)),
                pltpu.SemaphoreType.DMA((slots,)),
            ],
            compiler_params=pltpu.CompilerParams(
                collective_id=0, has_side_effects=True, vmem_limit_bytes=32 * 1024 * 1024
            ),
        )(
            pltpu.with_memory_space_constraint(queries, pltpu.HBM),
            pltpu.with_memory_space_constraint(key_value_pairs, pltpu.HBM),
            span_index,
            valid_count,
        )

    return jax.shard_map(
        shards,
        mesh=mesh,
        in_specs=(P("span", "seq", None), P("span", "seq", None), P("span"), P("span")),
        out_specs=P("span", "seq", None),
        check_vma=False,
    )
```

```python
import functools
import math

import jax
import jax.numpy as jnp
from jax import lax
from jax.experimental import pallas as pl
from jax.experimental.pallas import tpu as pltpu
from jax.sharding import PartitionSpec as P

MESH = pl.DeviceIdType.MESH
HEAD = 128
LIST = 3
KEYS = 128
HALF = KEYS // 2
META = 16
ROW_EXTRA = 128
SCALE = HEAD ** (-0.5) / math.log(2.0)
NO_MAX = -(2.0**100)
HIDDEN = -(2.0**101)
FAR = 100.0


TREES = (
    {-7: -4, -6: -5, -5: -4, -4: -1, -3: -4, -2: -1, -1: 3, 1: -2, 2: 1, 3: 0, 4: 3, 5: 3, 6: 5, 7: 5, 8: -7},
    {-7: -6, -6: -3, -5: -6, -4: -3, -3: 0, -2: -3, -1: 2, 1: -3, 2: 1, 3: 2, 4: 1, 5: 4, 6: 4, 7: 6, 8: -6},
)
DIRECT = (1, -1)
GROUPS = ((0, 1), (-1, 2), (-4, 4), (-2, 3), (-3, 5), (-7, -5), (6, -6), (8, 7))
EVENTS = (
    ((0, 1), (0, -1), (1, 1), (1, -1), (0, 3), (1, -3), (0, 2),),
    (),
    ((0, -2), (1, 2), (0, -4), (1, 4), (1, -4), (0, 4),),
    ((1, -2),),
    ((1, -6), (0, 5), (1, 3), (0, -3), (0, -5),),
    (),
    ((1, 5), (0, -7), (1, 6), (1, -7),),
    ((1, -5),),
    ((0, 6), (1, 8), (0, -6),),
    ((0, 7),),
    ((0, 8), (1, 7),),
    (),
    (),
    (),
    (),
)
CHILDREN = tuple(
    {parent: [child for child in tree if tree[child] == parent and child not in DIRECT] for parent in set(tree.values())} for tree in TREES
)


def hops(child, parent):
    return (child - parent + 8) % 16 - 8


def kernel(
    n_span, n_seq,
    q_hbm, kv_hbm, index_ref, count_ref, out_ref,
    kvbuf, metabuf, qbuf, place_buf, max_ref, sum_ref, acc_ref, part_buf, got_buf,
    a2a_send, a2a_recv, ring_send, chunk_recv, meta_recv,
):
    tokens = q_hbm.shape[1]
    half_spans = n_span // 2
    n_z = half_spans // 2
    span = lax.axis_index("span")
    seq = lax.axis_index("seq")
    half = lax.div(span, half_spans)
    slot = lax.rem(span, half_spans)
    z = lax.div(slot, 2)
    core = lax.rem(slot, 2)
    group = seq ^ half
    partner_span = (1 - half) * half_spans + slot
    sibling = (half * half_spans + z * 2 + (1 - core), seq)

    def z_at(offset):
        return lax.rem(z + offset + n_z, n_z)

    def along(offset):
        return (half * half_spans + z_at(offset) * 2 + core, seq)

    barrier = pltpu.get_barrier_semaphore()
    peers = [(span, seq ^ d) for d in range(1, n_seq)]
    peers += [(partner_span, seq ^ d) for d in range(n_seq)]
    steps = sorted({child - parent for tree in TREES for child, parent in tree.items()} | {abs(n) for n in DIRECT})
    steps = [s for s in steps if s > 0]
    peers += [along(sign * s) for s in steps for sign in (1, -1)]
    peers += [(along(n)[0], seq ^ d) for n in DIRECT for d in range(1, n_seq)]
    peers.append(sibling)
    for device in peers:
        pl.semaphore_signal(barrier, inc=1, device_id=device, device_id_type=MESH)

    index = index_ref[0].astype(jnp.float32)
    lane = lax.broadcasted_iota(jnp.int32, (1, 128), 1)
    metabuf[slot] = jnp.where(lane < count_ref[0], index, FAR)
    place_buf[0] = jnp.full((META, 128), index, jnp.float32).astype(jnp.bfloat16)

    pl.semaphore_wait(barrier, len(peers))

    def send(src, dst, send_sem, recv_sem, device):
        pltpu.make_async_remote_copy(
            src_ref=src, dst_ref=dst, send_sem=send_sem, recv_sem=recv_sem, device_id=device, device_id_type=MESH
        ).start()

    def wait(ref, sem):
        pltpu.make_async_copy(ref, ref, sem).wait()

    rows = pl.ds(pl.multiple_of(seq * tokens, tokens), tokens)

    def columns(start, size):
        return pl.ds(pl.multiple_of(start, 128), size)

    for n in DIRECT:
        send(metabuf.at[slot], metabuf.at[slot], ring_send.at[2], meta_recv.at[slot], along(n))
    own_chunk = lax.div(seq, n_seq // 2)
    for n in (0, *DIRECT):
        for d in range(n_seq):
            their = (seq ^ d) ^ half
            src = kv_hbm.at[0, :, columns(their * 256, 256)]
            dst = kvbuf.at[slot, rows, :]
            if n:
                send(src, dst, a2a_send.at[1], chunk_recv.at[own_chunk, slot], (along(n)[0], seq ^ d))
            elif d:
                send(src, dst, a2a_send.at[0], a2a_recv.at[own_chunk], (span, seq ^ d))
            else:
                pltpu.make_async_copy(src, dst, a2a_recv.at[own_chunk]).start()

    for d in range(n_seq):
        their = (seq ^ d) ^ half
        src = q_hbm.at[0, :, columns(their * (LIST * HEAD), LIST * HEAD)]
        dst = qbuf.at[0, rows, :]
        if d == 0:
            pltpu.make_async_copy(src, dst, a2a_recv.at[2]).start()
        else:
            send(src, dst, a2a_send.at[2], a2a_recv.at[2], (span, seq ^ d))
    for d in range(n_seq):
        their = (seq ^ d) ^ (1 - half)
        src = q_hbm.at[0, :, columns(their * (LIST * HEAD), LIST * HEAD)]
        send(src, qbuf.at[1, rows, :], a2a_send.at[3], a2a_recv.at[3], (partner_span, seq ^ d))

    send(place_buf.at[0], place_buf.at[1], a2a_send.at[4], a2a_recv.at[4], (partner_span, seq ^ 1))

    max_ref[...] = jnp.full(max_ref.shape, NO_MAX, jnp.float32)
    sum_ref[...] = jnp.zeros(sum_ref.shape, jnp.float32)
    acc_ref[...] = jnp.zeros(acc_ref.shape, jnp.float32)

    def chunk_of(chunk, which):
        return kvbuf.at[which, pl.ds(chunk * HALF, HALF), :]

    def pass_on(chunk, which, device):
        ref = chunk_of(chunk, which)
        send(ref, ref, ring_send.at[chunk], chunk_recv.at[chunk, which], device)
        if chunk == 0:
            send(metabuf.at[which], metabuf.at[which], ring_send.at[2], meta_recv.at[which], device)

    def wait_for(chunk, which):
        if chunk == 0:
            wait(metabuf.at[which], meta_recv.at[which])
        wait(chunk_of(chunk, which), chunk_recv.at[chunk, which])

    def hand_on(chunk, offset):
        which = z_at(-offset) * 2 + core
        for child in CHILDREN[chunk].get(offset, ()):
            pass_on(chunk, which, along(hops(child, offset)))
        pass_on(chunk, which, sibling)

    for chunk in range(2):
        wait(chunk_of(chunk, slot), a2a_recv.at[chunk])
        hand_on(chunk, 0)

    def attend(b, pairs):
        mine = place_buf[b].astype(jnp.float32)[:1]
        metas = [metabuf[which] for pair in pairs for which in pair]
        biases = [jnp.where(meta <= mine, 0.0, HIDDEN) for meta in metas]
        products = []
        for head in range(LIST):
            query = qbuf[b, :, head * HEAD : (head + 1) * HEAD]
            for pair in pairs:
                keys = jnp.concatenate([kvbuf[which, :, :HEAD] for which in pair], axis=0)
                products.append(
                    lax.dot_general(query, keys, (((1,), (1,)), ((), ())), preferred_element_type=jnp.float32)
                )
        weights = []
        for head in range(LIST):
            tile = b * LIST + head
            scores = []
            for i, bias in enumerate(biases):
                product = products[head * len(pairs) + i // 2]
                scores.append(product[:, i % 2 * KEYS : (i % 2 + 1) * KEYS] * SCALE + bias)
            old_max = max_ref[tile]
            top = functools.reduce(jnp.maximum, scores)
            new_max = jnp.maximum(old_max, jnp.max(top, axis=-1, keepdims=True))
            alpha = jnp.exp2(old_max - new_max)
            raw = [jnp.exp2(score - new_max) for score in scores]
            max_ref[tile] = new_max
            sum_ref[tile] = sum_ref[tile] * alpha + functools.reduce(jnp.add, raw)
            weights.append((alpha, [w.astype(jnp.bfloat16) for w in raw]))
        for head in range(LIST):
            tile = b * LIST + head
            alpha, raw = weights[head]
            total = acc_ref[tile] * alpha
            for i, pair in enumerate(pairs):
                values = jnp.concatenate([kvbuf[which, :, HEAD:] for which in pair], axis=0)
                total += jnp.dot(
                    jnp.concatenate(raw[2 * i : 2 * i + 2], axis=1), values, preferred_element_type=jnp.float32
                )
            acc_ref[tile] = total

    def finish(b):
        lane = lax.broadcasted_iota(jnp.int32, (KEYS, 128), 1)
        stats = jnp.zeros((KEYS, 128), jnp.float32)
        for head in range(LIST):
            tile = b * LIST + head
            top = max_ref[tile]
            sent_max = top.astype(jnp.bfloat16).astype(jnp.float32)
            factor = jnp.exp2(top - sent_max)
            total = jnp.sum(sum_ref[tile], axis=-1, keepdims=True) * factor
            high = total.astype(jnp.bfloat16).astype(jnp.float32)
            stats = jnp.where(lane == 3 * head, sent_max, stats)
            stats = jnp.where(lane == 3 * head + 1, high, stats)
            stats = jnp.where(lane == 3 * head + 2, total - high, stats)
            part_buf[b, :, head * HEAD : (head + 1) * HEAD] = (acc_ref[tile] * factor).astype(jnp.bfloat16)
        part_buf[b, :, LIST * HEAD :] = stats.astype(jnp.bfloat16)
        for d in range(n_seq):
            to = seq ^ d
            src = part_buf.at[b, pl.ds(pl.multiple_of(to * tokens, tokens), tokens), :]
            dst = got_buf.at[b, group]
            if b == 0 and d == 0:
                pltpu.make_async_copy(src, dst, a2a_recv.at[5]).start()
            else:
                device = (span if b == 0 else partner_span, to)
                send(src, dst, a2a_send.at[5 + b], a2a_recv.at[5 + b], device)

    def places_of(g):
        places = []
        for which in range(2):
            offset = GROUPS[0][which]
            for i in range(1, len(GROUPS)):
                offset = jnp.where(g == i, GROUPS[i][which], offset)
            places.append(z_at(-offset))
        return places

    def arrive(events):
        for chunk, offset in events:
            wait_for(chunk, z_at(-offset) * 2 + core)
            hand_on(chunk, offset)

    def wait_other(places):
        for place in places:
            for chunk in range(2):
                wait_for(chunk, place * 2 + 1 - core)

    def loop(i, carry):
        for at, events in enumerate(EVENTS[:-1]):
            if events:

                @pl.when(i == at)
                def _():
                    arrive(events)

        @pl.when(i == 0)
        def _():
            wait(qbuf.at[0], a2a_recv.at[2])
            wait(qbuf.at[1], a2a_recv.at[3])
            wait(place_buf.at[1], a2a_recv.at[4])

        places = places_of(lax.div(i, 2))

        @pl.when(lax.rem(i, 2) == 0)
        def _():
            wait_other(places)

        attend(1 - lax.rem(i, 2), [[place * 2, place * 2 + 1] for place in places])
        return carry

    lax.fori_loop(0, len(EVENTS) - 1, loop, 0)
    arrive(EVENTS[-1])
    places = [z_at(-offset) for offset in GROUPS[-1]]
    own = [[place * 2 + core for place in places]]
    others = [[place * 2 + 1 - core for place in places]]
    attend(1, own)
    attend(0, own)
    wait_other(places)
    attend(1, others)
    finish(1)
    attend(0, others)
    finish(0)

    for chunk in range(2):
        wait(kvbuf.at[pl.ds(0, half_spans - 1 - len(DIRECT)), pl.ds(0, HALF), :], ring_send.at[chunk])
    wait(metabuf.at[pl.ds(0, half_spans - 1)], ring_send.at[2])
    wait(kvbuf.at[0, pl.ds(0, (n_seq - 1) * tokens), :], a2a_send.at[0])
    if DIRECT:
        wait(kvbuf.at[pl.ds(0, len(DIRECT))], a2a_send.at[1])
    wait(qbuf.at[0, pl.ds(0, (n_seq - 1) * tokens), :], a2a_send.at[2])
    wait(qbuf.at[1], a2a_send.at[3])
    wait(place_buf.at[0], a2a_send.at[4])

    wait(got_buf.at[1], a2a_recv.at[6])
    wait(got_buf.at[0], a2a_recv.at[5])
    for g in range(n_seq):
        stats = [got_buf[b, g, :, LIST * HEAD :].astype(jnp.float32) for b in range(2)]
        for head in range(LIST):
            tops = [s[:, 3 * head : 3 * head + 1] for s in stats]
            totals = [s[:, 3 * head + 1 : 3 * head + 2] + s[:, 3 * head + 2 : 3 * head + 3] for s in stats]
            top = jnp.maximum(*tops)
            shares = [jnp.exp2(t - top) for t in tops]
            whole = shares[0] * totals[0] + shares[1] * totals[1]
            shares = [s / whole for s in shares]
            parts = [got_buf[b, g, :, head * HEAD : (head + 1) * HEAD].astype(jnp.float32) for b in range(2)]
            place = (g * LIST + head) * HEAD
            out_ref[0, :, place : place + HEAD] = (parts[0] * shares[0] + parts[1] * shares[1]).astype(jnp.bfloat16)
    wait(part_buf.at[0, pl.ds(0, (n_seq - 1) * tokens), :], a2a_send.at[5])
    wait(part_buf.at[1], a2a_send.at[6])


def solution(mesh):
    n_span, n_seq = mesh.shape["span"], mesh.shape["seq"]
    slots = n_span // 2

    def shards(queries, key_value_pairs, span_index, valid_count):
        tokens = queries.shape[1]
        return pl.pallas_call(
            functools.partial(kernel, n_span, n_seq),
            out_shape=jax.ShapeDtypeStruct(queries.shape, jnp.bfloat16),
            in_specs=[pl.BlockSpec(memory_space=pl.ANY)] * 2 + [pl.BlockSpec(memory_space=pltpu.SMEM)] * 2,
            out_specs=pl.BlockSpec(memory_space=pltpu.VMEM),
            scratch_shapes=[
                pltpu.VMEM((slots, KEYS, 2 * HEAD), jnp.bfloat16),
                pltpu.VMEM((slots, 1, 128), jnp.float32),
                pltpu.VMEM((2, KEYS, LIST * HEAD), jnp.bfloat16),
                pltpu.VMEM((2, META, 128), jnp.bfloat16),
                pltpu.VMEM((2 * LIST, KEYS, HEAD), jnp.float32),
                pltpu.VMEM((2 * LIST, KEYS, HEAD), jnp.float32),
                pltpu.VMEM((2 * LIST, KEYS, HEAD), jnp.float32),
                pltpu.VMEM((2, KEYS, LIST * HEAD + ROW_EXTRA), jnp.bfloat16),
                pltpu.VMEM((2, n_seq, tokens, LIST * HEAD + ROW_EXTRA), jnp.bfloat16),
                pltpu.SemaphoreType.DMA((7,)),
                pltpu.SemaphoreType.DMA((7,)),
                pltpu.SemaphoreType.DMA((3,)),
                pltpu.SemaphoreType.DMA((2, slots)),
                pltpu.SemaphoreType.DMA((slots,)),
            ],
            compiler_params=pltpu.CompilerParams(
                collective_id=0, has_side_effects=True, vmem_limit_bytes=32 * 1024 * 1024
            ),
        )(
            pltpu.with_memory_space_constraint(queries, pltpu.HBM),
            pltpu.with_memory_space_constraint(key_value_pairs, pltpu.HBM),
            span_index,
            valid_count,
        )

    return jax.shard_map(
        shards,
        mesh=mesh,
        in_specs=(P("span", "seq", None), P("span", "seq", None), P("span"), P("span")),
        out_specs=P("span", "seq", None),
        check_vma=False,
    )
```

```python
import functools
import math

import jax
import jax.numpy as jnp
from jax import lax
from jax.experimental import pallas as pl
from jax.experimental.pallas import tpu as pltpu
from jax.sharding import PartitionSpec as P

MESH = pl.DeviceIdType.MESH
HEAD = 128
LIST = 3
KEYS = 128
HALF = KEYS // 2
META = 16
ROW_EXTRA = 128
SCALE = HEAD ** (-0.5) / math.log(2.0)
NO_MAX = -(2.0**100)
HIDDEN = -(2.0**101)
FAR = 100.0


TREES = (
    {-7: -4, -6: -5, -5: -4, -4: -1, -3: -4, -2: -1, -1: 3, 1: -2, 2: 1, 3: 0, 4: 3, 5: 3, 6: 5, 7: 5, 8: -7},
    {-7: -6, -6: -3, -5: -6, -4: -3, -3: 0, -2: -3, -1: 2, 1: -3, 2: 1, 3: 2, 4: 1, 5: 4, 6: 4, 7: 6, 8: -6},
)
DIRECT = (1, -1)
GROUPS = ((0, 1), (-1, 2), (-4, 4), (-2, 3), (-3, 5), (-7, -5), (6, -6), (8, 7))
EVENTS = (
    ((0, 1), (0, -1), (1, 1), (1, -1), (0, 3), (1, -3), (0, 2),),
    (),
    ((0, -2), (1, 2), (0, -4), (1, 4), (1, -4), (0, 4),),
    ((1, -2),),
    ((1, -6), (0, 5), (1, 3), (0, -3), (0, -5),),
    (),
    ((1, 5), (0, -7), (1, 6), (1, -7),),
    ((1, -5),),
    ((0, 6), (1, 8), (0, -6),),
    ((0, 7),),
    ((0, 8), (1, 7),),
    (),
    (),
    (),
    (),
)
CHILDREN = tuple(
    {parent: [child for child in tree if tree[child] == parent and child not in DIRECT] for parent in set(tree.values())} for tree in TREES
)


def hops(child, parent):
    return (child - parent + 8) % 16 - 8


def kernel(
    n_span, n_seq,
    q_hbm, kv_hbm, index_ref, count_ref, out_ref,
    kvbuf, metabuf, qbuf, place_buf, max_ref, sum_ref, acc_ref, part_buf, got_buf,
    a2a_send, a2a_recv, ring_send, chunk_recv, meta_recv,
):
    tokens = q_hbm.shape[1]
    half_spans = n_span // 2
    n_z = half_spans // 2
    span = lax.axis_index("span")
    seq = lax.axis_index("seq")
    half = lax.div(span, half_spans)
    slot = lax.rem(span, half_spans)
    z = lax.div(slot, 2)
    core = lax.rem(slot, 2)
    group = seq ^ half
    partner_span = (1 - half) * half_spans + slot
    sibling = (half * half_spans + z * 2 + (1 - core), seq)

    far_first = sorted(range(n_seq), key=lambda d: -(d // 2 == 2) * 4 - d % 2 - (d > 1) * 2)

    def z_at(offset):
        return lax.rem(z + offset + n_z, n_z)

    def along(offset):
        return (half * half_spans + z_at(offset) * 2 + core, seq)

    barrier = pltpu.get_barrier_semaphore()
    peers = [(span, seq ^ d) for d in range(1, n_seq)]
    peers += [(partner_span, seq ^ d) for d in range(n_seq)]
    steps = sorted({child - parent for tree in TREES for child, parent in tree.items()} | {abs(n) for n in DIRECT})
    steps = [s for s in steps if s > 0]
    peers += [along(sign * s) for s in steps for sign in (1, -1)]
    peers += [(along(n)[0], seq ^ d) for n in DIRECT for d in range(1, n_seq)]
    peers.append(sibling)
    for device in peers:
        pl.semaphore_signal(barrier, inc=1, device_id=device, device_id_type=MESH)

    index = index_ref[0].astype(jnp.float32)
    lane = lax.broadcasted_iota(jnp.int32, (1, 128), 1)
    metabuf[slot] = jnp.where(lane < count_ref[0], index, FAR)
    place_buf[0] = jnp.full((META, 128), index, jnp.float32).astype(jnp.bfloat16)

    pl.semaphore_wait(barrier, len(peers))

    def send(src, dst, send_sem, recv_sem, device):
        pltpu.make_async_remote_copy(
            src_ref=src, dst_ref=dst, send_sem=send_sem, recv_sem=recv_sem, device_id=device, device_id_type=MESH
        ).start()

    def wait(ref, sem):
        pltpu.make_async_copy(ref, ref, sem).wait()

    rows = pl.ds(pl.multiple_of(seq * tokens, tokens), tokens)

    def columns(start, size):
        return pl.ds(pl.multiple_of(start, 128), size)

    for n in DIRECT:
        send(metabuf.at[slot], metabuf.at[slot], ring_send.at[2], meta_recv.at[slot], along(n))
    own_chunk = lax.div(seq, n_seq // 2)
    for n in (0, *DIRECT):
        for d in far_first:
            their = (seq ^ d) ^ half
            src = kv_hbm.at[0, :, columns(their * 256, 256)]
            dst = kvbuf.at[slot, rows, :]
            if n:
                send(src, dst, a2a_send.at[1], chunk_recv.at[own_chunk, slot], (along(n)[0], seq ^ d))
            elif d:
                send(src, dst, a2a_send.at[0], a2a_recv.at[own_chunk], (span, seq ^ d))
            else:
                pltpu.make_async_copy(src, dst, a2a_recv.at[own_chunk]).start()

    for d in range(n_seq):
        their = (seq ^ d) ^ half
        src = q_hbm.at[0, :, columns(their * (LIST * HEAD), LIST * HEAD)]
        dst = qbuf.at[0, rows, :]
        if d == 0:
            pltpu.make_async_copy(src, dst, a2a_recv.at[2]).start()
        else:
            send(src, dst, a2a_send.at[2], a2a_recv.at[2], (span, seq ^ d))
    for d in range(n_seq):
        their = (seq ^ d) ^ (1 - half)
        src = q_hbm.at[0, :, columns(their * (LIST * HEAD), LIST * HEAD)]
        send(src, qbuf.at[1, rows, :], a2a_send.at[3], a2a_recv.at[3], (partner_span, seq ^ d))

    send(place_buf.at[0], place_buf.at[1], a2a_send.at[4], a2a_recv.at[4], (partner_span, seq ^ 1))

    max_ref[...] = jnp.full(max_ref.shape, NO_MAX, jnp.float32)
    sum_ref[...] = jnp.zeros(sum_ref.shape, jnp.float32)
    acc_ref[...] = jnp.zeros(acc_ref.shape, jnp.float32)

    def chunk_of(chunk, which):
        return kvbuf.at[which, pl.ds(chunk * HALF, HALF), :]

    def pass_on(chunk, which, device):
        ref = chunk_of(chunk, which)
        send(ref, ref, ring_send.at[chunk], chunk_recv.at[chunk, which], device)
        if chunk == 0:
            send(metabuf.at[which], metabuf.at[which], ring_send.at[2], meta_recv.at[which], device)

    def wait_for(chunk, which):
        if chunk == 0:
            wait(metabuf.at[which], meta_recv.at[which])
        wait(chunk_of(chunk, which), chunk_recv.at[chunk, which])

    def hand_on(chunk, offset):
        which = z_at(-offset) * 2 + core
        for child in CHILDREN[chunk].get(offset, ()):
            pass_on(chunk, which, along(hops(child, offset)))
        pass_on(chunk, which, sibling)

    for chunk in range(2):
        wait(chunk_of(chunk, slot), a2a_recv.at[chunk])
        hand_on(chunk, 0)

    def attend(b, pairs):
        mine = place_buf[b].astype(jnp.float32)[:1]
        metas = [metabuf[which] for pair in pairs for which in pair]
        biases = [jnp.where(meta <= mine, 0.0, HIDDEN) for meta in metas]
        products = []
        for head in range(LIST):
            query = qbuf[b, :, head * HEAD : (head + 1) * HEAD]
            for pair in pairs:
                keys = jnp.concatenate([kvbuf[which, :, :HEAD] for which in pair], axis=0)
                products.append(
                    lax.dot_general(query, keys, (((1,), (1,)), ((), ())), preferred_element_type=jnp.float32)
                )
        weights = []
        for head in range(LIST):
            tile = b * LIST + head
            scores = []
            for i, bias in enumerate(biases):
                product = products[head * len(pairs) + i // 2]
                scores.append(product[:, i % 2 * KEYS : (i % 2 + 1) * KEYS] * SCALE + bias)
            old_max = max_ref[tile]
            top = functools.reduce(jnp.maximum, scores)
            new_max = jnp.maximum(old_max, jnp.max(top, axis=-1, keepdims=True))
            alpha = jnp.exp2(old_max - new_max)
            raw = [jnp.exp2(score - new_max) for score in scores]
            max_ref[tile] = new_max
            sum_ref[tile] = sum_ref[tile] * alpha + functools.reduce(jnp.add, raw)
            weights.append((alpha, [w.astype(jnp.bfloat16) for w in raw]))
        for head in range(LIST):
            tile = b * LIST + head
            alpha, raw = weights[head]
            total = acc_ref[tile] * alpha
            for i, pair in enumerate(pairs):
                values = jnp.concatenate([kvbuf[which, :, HEAD:] for which in pair], axis=0)
                total += jnp.dot(
                    jnp.concatenate(raw[2 * i : 2 * i + 2], axis=1), values, preferred_element_type=jnp.float32
                )
            acc_ref[tile] = total

    def finish(b):
        lane = lax.broadcasted_iota(jnp.int32, (KEYS, 128), 1)
        stats = jnp.zeros((KEYS, 128), jnp.float32)
        for head in range(LIST):
            tile = b * LIST + head
            top = max_ref[tile]
            sent_max = top.astype(jnp.bfloat16).astype(jnp.float32)
            factor = jnp.exp2(top - sent_max)
            total = jnp.sum(sum_ref[tile], axis=-1, keepdims=True) * factor
            high = total.astype(jnp.bfloat16).astype(jnp.float32)
            stats = jnp.where(lane == 3 * head, sent_max, stats)
            stats = jnp.where(lane == 3 * head + 1, high, stats)
            stats = jnp.where(lane == 3 * head + 2, total - high, stats)
            part_buf[b, :, head * HEAD : (head + 1) * HEAD] = (acc_ref[tile] * factor).astype(jnp.bfloat16)
        part_buf[b, :, LIST * HEAD :] = stats.astype(jnp.bfloat16)
        for d in far_first:
            to = seq ^ d
            src = part_buf.at[b, pl.ds(pl.multiple_of(to * tokens, tokens), tokens), :]
            dst = got_buf.at[b, group]
            if b == 0 and d == 0:
                pltpu.make_async_copy(src, dst, a2a_recv.at[5]).start()
            else:
                device = (span if b == 0 else partner_span, to)
                send(src, dst, a2a_send.at[5 + b], a2a_recv.at[5 + b], device)

    def places_of(g):
        places = []
        for which in range(2):
            offset = GROUPS[0][which]
            for i in range(1, len(GROUPS)):
                offset = jnp.where(g == i, GROUPS[i][which], offset)
            places.append(z_at(-offset))
        return places

    def arrive(events):
        for chunk, offset in events:
            wait_for(chunk, z_at(-offset) * 2 + core)
            hand_on(chunk, offset)

    def wait_other(places):
        for place in places:
            for chunk in range(2):
                wait_for(chunk, place * 2 + 1 - core)

    def loop(i, carry):
        for at, events in enumerate(EVENTS[:-1]):
            if events:

                @pl.when(i == at)
                def _():
                    arrive(events)

        @pl.when(i == 0)
        def _():
            wait(qbuf.at[0], a2a_recv.at[2])
            wait(qbuf.at[1], a2a_recv.at[3])
            wait(place_buf.at[1], a2a_recv.at[4])

        places = places_of(lax.div(i, 2))

        @pl.when(lax.rem(i, 2) == 0)
        def _():
            wait_other(places)

        attend(1 - lax.rem(i, 2), [[place * 2, place * 2 + 1] for place in places])
        return carry

    lax.fori_loop(0, len(EVENTS) - 1, loop, 0)
    arrive(EVENTS[-1])
    places = [z_at(-offset) for offset in GROUPS[-1]]
    own = [[place * 2 + core for place in places]]
    others = [[place * 2 + 1 - core for place in places]]
    attend(1, own)
    attend(0, own)
    wait_other(places)
    attend(1, others)
    finish(1)
    attend(0, others)
    finish(0)

    for chunk in range(2):
        wait(kvbuf.at[pl.ds(0, half_spans - 1 - len(DIRECT)), pl.ds(0, HALF), :], ring_send.at[chunk])
    wait(metabuf.at[pl.ds(0, half_spans - 1)], ring_send.at[2])
    wait(kvbuf.at[0, pl.ds(0, (n_seq - 1) * tokens), :], a2a_send.at[0])
    if DIRECT:
        wait(kvbuf.at[pl.ds(0, len(DIRECT))], a2a_send.at[1])
    wait(qbuf.at[0, pl.ds(0, (n_seq - 1) * tokens), :], a2a_send.at[2])
    wait(qbuf.at[1], a2a_send.at[3])
    wait(place_buf.at[0], a2a_send.at[4])

    wait(got_buf.at[1], a2a_recv.at[6])
    wait(got_buf.at[0], a2a_recv.at[5])
    for g in range(n_seq):
        stats = [got_buf[b, g, :, LIST * HEAD :].astype(jnp.float32) for b in range(2)]
        for head in range(LIST):
            tops = [s[:, 3 * head : 3 * head + 1] for s in stats]
            totals = [s[:, 3 * head + 1 : 3 * head + 2] + s[:, 3 * head + 2 : 3 * head + 3] for s in stats]
            top = jnp.maximum(*tops)
            shares = [jnp.exp2(t - top) for t in tops]
            whole = shares[0] * totals[0] + shares[1] * totals[1]
            shares = [s / whole for s in shares]
            parts = [got_buf[b, g, :, head * HEAD : (head + 1) * HEAD].astype(jnp.float32) for b in range(2)]
            place = (g * LIST + head) * HEAD
            out_ref[0, :, place : place + HEAD] = (parts[0] * shares[0] + parts[1] * shares[1]).astype(jnp.bfloat16)
    wait(part_buf.at[0, pl.ds(0, (n_seq - 1) * tokens), :], a2a_send.at[5])
    wait(part_buf.at[1], a2a_send.at[6])


def solution(mesh):
    n_span, n_seq = mesh.shape["span"], mesh.shape["seq"]
    slots = n_span // 2

    def shards(queries, key_value_pairs, span_index, valid_count):
        tokens = queries.shape[1]
        return pl.pallas_call(
            functools.partial(kernel, n_span, n_seq),
            out_shape=jax.ShapeDtypeStruct(queries.shape, jnp.bfloat16),
            in_specs=[pl.BlockSpec(memory_space=pl.ANY)] * 2 + [pl.BlockSpec(memory_space=pltpu.SMEM)] * 2,
            out_specs=pl.BlockSpec(memory_space=pltpu.VMEM),
            scratch_shapes=[
                pltpu.VMEM((slots, KEYS, 2 * HEAD), jnp.bfloat16),
                pltpu.VMEM((slots, 1, 128), jnp.float32),
                pltpu.VMEM((2, KEYS, LIST * HEAD), jnp.bfloat16),
                pltpu.VMEM((2, META, 128), jnp.bfloat16),
                pltpu.VMEM((2 * LIST, KEYS, HEAD), jnp.float32),
                pltpu.VMEM((2 * LIST, KEYS, HEAD), jnp.float32),
                pltpu.VMEM((2 * LIST, KEYS, HEAD), jnp.float32),
                pltpu.VMEM((2, KEYS, LIST * HEAD + ROW_EXTRA), jnp.bfloat16),
                pltpu.VMEM((2, n_seq, tokens, LIST * HEAD + ROW_EXTRA), jnp.bfloat16),
                pltpu.SemaphoreType.DMA((7,)),
                pltpu.SemaphoreType.DMA((7,)),
                pltpu.SemaphoreType.DMA((3,)),
                pltpu.SemaphoreType.DMA((2, slots)),
                pltpu.SemaphoreType.DMA((slots,)),
            ],
            compiler_params=pltpu.CompilerParams(
                collective_id=0, has_side_effects=True, vmem_limit_bytes=32 * 1024 * 1024
            ),
        )(
            pltpu.with_memory_space_constraint(queries, pltpu.HBM),
            pltpu.with_memory_space_constraint(key_value_pairs, pltpu.HBM),
            span_index,
            valid_count,
        )

    return jax.shard_map(
        shards,
        mesh=mesh,
        in_specs=(P("span", "seq", None), P("span", "seq", None), P("span"), P("span")),
        out_specs=P("span", "seq", None),
        check_vma=False,
    )
```

```python
import functools
import math

import jax
import jax.numpy as jnp
from jax import lax
from jax.experimental import pallas as pl
from jax.experimental.pallas import tpu as pltpu
from jax.sharding import PartitionSpec as P

MESH = pl.DeviceIdType.MESH
HEAD = 128
LIST = 3
KEYS = 128
HALF = KEYS // 2
META = 16
ROW_EXTRA = 128
SCALE = HEAD ** (-0.5) / math.log(2.0)
NO_MAX = -(2.0**100)
HIDDEN = -(2.0**101)
FAR = 100.0


TREES = (
    {-7: -4, -6: -5, -5: -4, -4: -1, -3: -4, -2: -1, -1: 3, 1: -2, 2: 1, 3: 0, 4: 3, 5: 3, 6: 5, 7: 5, 8: -7},
    {-7: -6, -6: -3, -5: -6, -4: -3, -3: 0, -2: -3, -1: 2, 1: -3, 2: 1, 3: 2, 4: 1, 5: 4, 6: 4, 7: 6, 8: -6},
)
DIRECT = (1, -1)
GROUPS = ((0, 1), (-1, 2), (-4, 4), (-2, 3), (-3, 5), (-7, -5), (6, -6), (8, 7))
EVENTS = (
    ((0, 1), (0, -1), (1, 1), (1, -1), (0, 3), (1, -3), (0, 2),),
    (),
    ((0, -2), (1, 2), (0, -4), (1, 4), (1, -4), (0, 4),),
    ((1, -2),),
    ((1, -6), (0, 5), (1, 3), (0, -3), (0, -5),),
    (),
    ((1, 5), (0, -7), (1, 6), (1, -7),),
    ((1, -5),),
    ((0, 6), (1, 8), (0, -6),),
    ((0, 7),),
    ((0, 8),),
    ((1, 7),),
    (),
    (),
    (),
)
CHILDREN = tuple(
    {parent: [child for child in tree if tree[child] == parent and child not in DIRECT] for parent in set(tree.values())} for tree in TREES
)


def hops(child, parent):
    return (child - parent + 8) % 16 - 8


def kernel(
    n_span, n_seq,
    q_hbm, kv_hbm, index_ref, count_ref, out_ref,
    kvbuf, metabuf, qbuf, place_buf, max_ref, sum_ref, acc_ref, part_buf, got_buf,
    a2a_send, a2a_recv, ring_send, chunk_recv, meta_recv,
):
    tokens = q_hbm.shape[1]
    half_spans = n_span // 2
    n_z = half_spans // 2
    span = lax.axis_index("span")
    seq = lax.axis_index("seq")
    half = lax.div(span, half_spans)
    slot = lax.rem(span, half_spans)
    z = lax.div(slot, 2)
    core = lax.rem(slot, 2)
    group = seq ^ half
    partner_span = (1 - half) * half_spans + slot
    sibling = (half * half_spans + z * 2 + (1 - core), seq)

    far_first = sorted(range(n_seq), key=lambda d: -(d // 2 == 2) * 4 - d % 2 - (d > 1) * 2)

    def z_at(offset):
        return lax.rem(z + offset + n_z, n_z)

    def along(offset):
        return (half * half_spans + z_at(offset) * 2 + core, seq)

    barrier = pltpu.get_barrier_semaphore()
    peers = [(span, seq ^ d) for d in range(1, n_seq)]
    peers += [(partner_span, seq ^ d) for d in range(n_seq)]
    steps = sorted({child - parent for tree in TREES for child, parent in tree.items()} | {abs(n) for n in DIRECT})
    steps = [s for s in steps if s > 0]
    peers += [along(sign * s) for s in steps for sign in (1, -1)]
    peers += [(along(n)[0], seq ^ d) for n in DIRECT for d in range(1, n_seq)]
    peers.append(sibling)
    for device in peers:
        pl.semaphore_signal(barrier, inc=1, device_id=device, device_id_type=MESH)

    index = index_ref[0].astype(jnp.float32)
    lane = lax.broadcasted_iota(jnp.int32, (1, 128), 1)
    metabuf[slot] = jnp.where(lane < count_ref[0], index, FAR)
    place_buf[0] = jnp.full((META, 128), index, jnp.float32).astype(jnp.bfloat16)

    pl.semaphore_wait(barrier, len(peers))

    def send(src, dst, send_sem, recv_sem, device):
        pltpu.make_async_remote_copy(
            src_ref=src, dst_ref=dst, send_sem=send_sem, recv_sem=recv_sem, device_id=device, device_id_type=MESH
        ).start()

    def wait(ref, sem):
        pltpu.make_async_copy(ref, ref, sem).wait()

    rows = pl.ds(pl.multiple_of(seq * tokens, tokens), tokens)

    def columns(start, size):
        return pl.ds(pl.multiple_of(start, 128), size)

    for n in DIRECT:
        send(metabuf.at[slot], metabuf.at[slot], ring_send.at[2], meta_recv.at[slot], along(n))
    own_chunk = lax.div(seq, n_seq // 2)
    for n in (0, *DIRECT):
        for d in far_first:
            their = (seq ^ d) ^ half
            src = kv_hbm.at[0, :, columns(their * 256, 256)]
            dst = kvbuf.at[slot, rows, :]
            if n:
                send(src, dst, a2a_send.at[1], chunk_recv.at[own_chunk, slot], (along(n)[0], seq ^ d))
            elif d:
                send(src, dst, a2a_send.at[0], a2a_recv.at[own_chunk], (span, seq ^ d))
            else:
                pltpu.make_async_copy(src, dst, a2a_recv.at[own_chunk]).start()

    for d in range(n_seq):
        their = (seq ^ d) ^ half
        src = q_hbm.at[0, :, columns(their * (LIST * HEAD), LIST * HEAD)]
        dst = qbuf.at[0, rows, :]
        if d == 0:
            pltpu.make_async_copy(src, dst, a2a_recv.at[2]).start()
        else:
            send(src, dst, a2a_send.at[2], a2a_recv.at[2], (span, seq ^ d))
    for d in range(n_seq):
        their = (seq ^ d) ^ (1 - half)
        src = q_hbm.at[0, :, columns(their * (LIST * HEAD), LIST * HEAD)]
        send(src, qbuf.at[1, rows, :], a2a_send.at[3], a2a_recv.at[3], (partner_span, seq ^ d))

    send(place_buf.at[0], place_buf.at[1], a2a_send.at[4], a2a_recv.at[4], (partner_span, seq ^ 1))

    max_ref[...] = jnp.full(max_ref.shape, NO_MAX, jnp.float32)
    sum_ref[...] = jnp.zeros(sum_ref.shape, jnp.float32)
    acc_ref[...] = jnp.zeros(acc_ref.shape, jnp.float32)

    def chunk_of(chunk, which):
        return kvbuf.at[which, pl.ds(chunk * HALF, HALF), :]

    def pass_on(chunk, which, device):
        ref = chunk_of(chunk, which)
        send(ref, ref, ring_send.at[chunk], chunk_recv.at[chunk, which], device)
        if chunk == 0:
            send(metabuf.at[which], metabuf.at[which], ring_send.at[2], meta_recv.at[which], device)

    def wait_for(chunk, which):
        if chunk == 0:
            wait(metabuf.at[which], meta_recv.at[which])
        wait(chunk_of(chunk, which), chunk_recv.at[chunk, which])

    def hand_on(chunk, offset):
        which = z_at(-offset) * 2 + core
        for child in CHILDREN[chunk].get(offset, ()):
            pass_on(chunk, which, along(hops(child, offset)))
        pass_on(chunk, which, sibling)

    for chunk in range(2):
        wait(chunk_of(chunk, slot), a2a_recv.at[chunk])
        hand_on(chunk, 0)

    def attend(spans, pairs):
        metas = [metabuf[which] for pair in pairs for which in pair]
        mine = [place_buf[b].astype(jnp.float32)[:1] for b in spans]
        biases = [[jnp.where(meta <= own, 0.0, HIDDEN) for meta in metas] for own in mine]
        work = [(i, b, head) for i, b in enumerate(spans) for head in range(LIST)]
        keys = [jnp.concatenate([kvbuf[which, :, :HEAD] for which in pair], axis=0) for pair in pairs]
        values = [jnp.concatenate([kvbuf[which, :, HEAD:] for which in pair], axis=0) for pair in pairs]
        products = []
        for _, b, head in work:
            query = qbuf[b, :, head * HEAD : (head + 1) * HEAD]
            products.append([
                lax.dot_general(query, k, (((1,), (1,)), ((), ())), preferred_element_type=jnp.float32) for k in keys
            ])
        weights = []
        for (i, b, head), product in zip(work, products):
            tile = b * LIST + head
            scores = [
                product[j // 2][:, j % 2 * KEYS : (j % 2 + 1) * KEYS] * SCALE + bias for j, bias in enumerate(biases[i])
            ]
            old_max = max_ref[tile]
            top = functools.reduce(jnp.maximum, scores)
            new_max = jnp.maximum(old_max, jnp.max(top, axis=-1, keepdims=True))
            alpha = jnp.exp2(old_max - new_max)
            raw = [jnp.exp2(score - new_max) for score in scores]
            max_ref[tile] = new_max
            sum_ref[tile] = sum_ref[tile] * alpha + functools.reduce(jnp.add, raw)
            weights.append((alpha, [w.astype(jnp.bfloat16) for w in raw]))
        for (_, b, head), (alpha, raw) in zip(work, weights):
            tile = b * LIST + head
            total = acc_ref[tile] * alpha
            for j, v in enumerate(values):
                total += jnp.dot(
                    jnp.concatenate(raw[2 * j : 2 * j + 2], axis=1), v, preferred_element_type=jnp.float32
                )
            acc_ref[tile] = total

    def finish(b):
        lane = lax.broadcasted_iota(jnp.int32, (KEYS, 128), 1)
        stats = jnp.zeros((KEYS, 128), jnp.float32)
        for head in range(LIST):
            tile = b * LIST + head
            top = max_ref[tile]
            sent_max = top.astype(jnp.bfloat16).astype(jnp.float32)
            factor = jnp.exp2(top - sent_max)
            total = jnp.sum(sum_ref[tile], axis=-1, keepdims=True) * factor
            high = total.astype(jnp.bfloat16).astype(jnp.float32)
            stats = jnp.where(lane == 3 * head, sent_max, stats)
            stats = jnp.where(lane == 3 * head + 1, high, stats)
            stats = jnp.where(lane == 3 * head + 2, total - high, stats)
            part_buf[b, :, head * HEAD : (head + 1) * HEAD] = (acc_ref[tile] * factor).astype(jnp.bfloat16)
        part_buf[b, :, LIST * HEAD :] = stats.astype(jnp.bfloat16)
        for d in far_first:
            to = seq ^ d
            src = part_buf.at[b, pl.ds(pl.multiple_of(to * tokens, tokens), tokens), :]
            dst = got_buf.at[b, group]
            if b == 0 and d == 0:
                pltpu.make_async_copy(src, dst, a2a_recv.at[5]).start()
            else:
                device = (span if b == 0 else partner_span, to)
                send(src, dst, a2a_send.at[5 + b], a2a_recv.at[5 + b], device)

    def places_of(g):
        places = []
        for which in range(2):
            offset = GROUPS[0][which]
            for i in range(1, len(GROUPS)):
                offset = jnp.where(g == i, GROUPS[i][which], offset)
            places.append(z_at(-offset))
        return places

    def arrive(events):
        for chunk, offset in events:
            wait_for(chunk, z_at(-offset) * 2 + core)
            hand_on(chunk, offset)

    def wait_other(places):
        for place in places:
            for chunk in range(2):
                wait_for(chunk, place * 2 + 1 - core)

    def loop(i, carry):
        for at, events in enumerate(EVENTS[:-1]):
            if events:

                @pl.when(i == at)
                def _():
                    arrive(events)

        @pl.when(i == 0)
        def _():
            wait(qbuf.at[0], a2a_recv.at[2])
            wait(qbuf.at[1], a2a_recv.at[3])
            wait(place_buf.at[1], a2a_recv.at[4])

        places = places_of(lax.div(i, 2))

        @pl.when(lax.rem(i, 2) == 0)
        def _():
            wait_other(places)

        attend([1 - lax.rem(i, 2)], [[place * 2, place * 2 + 1] for place in places])
        return carry

    lax.fori_loop(0, len(EVENTS) - 1, loop, 0)
    arrive(EVENTS[-1])
    places = [z_at(-offset) for offset in GROUPS[-1]]
    own = [[place * 2 + core for place in places]]
    others = [[place * 2 + 1 - core for place in places]]
    attend([1, 0], own)
    wait_other(places)
    attend([1, 0], others)
    finish(1)
    finish(0)

    for chunk in range(2):
        wait(kvbuf.at[pl.ds(0, half_spans - 1 - len(DIRECT)), pl.ds(0, HALF), :], ring_send.at[chunk])
    wait(metabuf.at[pl.ds(0, half_spans - 1)], ring_send.at[2])
    wait(kvbuf.at[0, pl.ds(0, (n_seq - 1) * tokens), :], a2a_send.at[0])
    if DIRECT:
        wait(kvbuf.at[pl.ds(0, len(DIRECT))], a2a_send.at[1])
    wait(qbuf.at[0, pl.ds(0, (n_seq - 1) * tokens), :], a2a_send.at[2])
    wait(qbuf.at[1], a2a_send.at[3])
    wait(place_buf.at[0], a2a_send.at[4])

    wait(got_buf.at[1], a2a_recv.at[6])
    wait(got_buf.at[0], a2a_recv.at[5])
    for g in range(n_seq):
        tops = [got_buf[b, g, :, LIST * HEAD :].astype(jnp.float32) for b in range(2)]
        totals = [pltpu.roll(t, 127, 1) + pltpu.roll(t, 126, 1) for t in tops]
        top = jnp.maximum(*tops)
        shares = [jnp.exp2(t - top) for t in tops]
        whole = shares[0] * totals[0] + shares[1] * totals[1]
        shares = [s / whole for s in shares]
        for head in range(LIST):
            mine = [s[:, 3 * head : 3 * head + 1] for s in shares]
            parts = [got_buf[b, g, :, head * HEAD : (head + 1) * HEAD].astype(jnp.float32) for b in range(2)]
            place = (g * LIST + head) * HEAD
            out_ref[0, :, place : place + HEAD] = (parts[0] * mine[0] + parts[1] * mine[1]).astype(jnp.bfloat16)
    wait(part_buf.at[0, pl.ds(0, (n_seq - 1) * tokens), :], a2a_send.at[5])
    wait(part_buf.at[1], a2a_send.at[6])


def solution(mesh):
    n_span, n_seq = mesh.shape["span"], mesh.shape["seq"]
    slots = n_span // 2

    def shards(queries, key_value_pairs, span_index, valid_count):
        tokens = queries.shape[1]
        return pl.pallas_call(
            functools.partial(kernel, n_span, n_seq),
            out_shape=jax.ShapeDtypeStruct(queries.shape, jnp.bfloat16),
            in_specs=[pl.BlockSpec(memory_space=pl.ANY)] * 2 + [pl.BlockSpec(memory_space=pltpu.SMEM)] * 2,
            out_specs=pl.BlockSpec(memory_space=pltpu.VMEM),
            scratch_shapes=[
                pltpu.VMEM((slots, KEYS, 2 * HEAD), jnp.bfloat16),
                pltpu.VMEM((slots, 1, 128), jnp.float32),
                pltpu.VMEM((2, KEYS, LIST * HEAD), jnp.bfloat16),
                pltpu.VMEM((2, META, 128), jnp.bfloat16),
                pltpu.VMEM((2 * LIST, KEYS, HEAD), jnp.float32),
                pltpu.VMEM((2 * LIST, KEYS, HEAD), jnp.float32),
                pltpu.VMEM((2 * LIST, KEYS, HEAD), jnp.float32),
                pltpu.VMEM((2, KEYS, LIST * HEAD + ROW_EXTRA), jnp.bfloat16),
                pltpu.VMEM((2, n_seq, tokens, LIST * HEAD + ROW_EXTRA), jnp.bfloat16),
                pltpu.SemaphoreType.DMA((7,)),
                pltpu.SemaphoreType.DMA((7,)),
                pltpu.SemaphoreType.DMA((3,)),
                pltpu.SemaphoreType.DMA((2, slots)),
                pltpu.SemaphoreType.DMA((slots,)),
            ],
            compiler_params=pltpu.CompilerParams(
                collective_id=0, has_side_effects=True, vmem_limit_bytes=32 * 1024 * 1024
            ),
        )(
            pltpu.with_memory_space_constraint(queries, pltpu.HBM),
            pltpu.with_memory_space_constraint(key_value_pairs, pltpu.HBM),
            span_index,
            valid_count,
        )

    return jax.shard_map(
        shards,
        mesh=mesh,
        in_specs=(P("span", "seq", None), P("span", "seq", None), P("span"), P("span")),
        out_specs=P("span", "seq", None),
        check_vma=False,
    )
```
